256 devices in a mesh: seq: 256 (over y, z, x, core).
Axes of the slice: x: 4, y: 4, z: 8, core: 2. Of those that a mesh axis runs over, the one named last changes fastest.
Arguments:
- queries: bfloat16 [65536, 768], P('seq'), may hold values from -4 to 4
- key_states: bfloat16 [65536, 768], P('seq'), may hold values from -4 to 4
- value_states: bfloat16 [65536, 768], P('seq'), may hold values from -6 to 6
- cotangent: bfloat16 [65536, 768], P('seq'), may hold values from -6 to 6
- offsets: int32 [3, 16], replicated, may hold values from 0 to 255, as said below
Outputs:
- attended: bfloat16 [65536, 768], P('seq')
- grad_query: bfloat16 [65536, 768], P('seq')
- grad_keys: bfloat16 [65536, 768], P('seq')
- grad_values: bfloat16 [65536, 768], P('seq')
The draws below stay inside these ranges and needn't reach their ends.
Inputs may be any that keep to these rules, and one draw needn't show every extreme that they name: Row b of offsets (b = 0, 1, 2) holds values below the dilation of branch b + 2 (8, 64, 256); every row holds a zero and its dilation minus one.
All inputs are finite; a program needn't handle non-finite values.
Results may differ from the reference program's by a relative error of at most 0.0033.
The reference program's roundings to bfloat16 on the way count: a program that leaves them out, or rounds other values in their place, can miss the bound.
Values may be sent and summed in bfloat16 or wider, within the bound.
No kernel may reach another device: no remote copies, remote signals or barrier semaphores. Data moves between devices by JAX's collectives and lax.ppermute only.
A program may use at most 128 MiB of HBM per device.

```python
import jax
import jax.numpy as jnp
from jax import lax

D = 768
HEAD_TOTAL = 16
DILATION_TWO = 8
DILATION_THREE = 64
DILATION_FOUR = 256
SEQ = 65536
SEGMENT_ONE = 512
SEGMENT_TWO = 4096
SEGMENT_THREE = 32768
SEGMENT_FOUR = 65536


def draw_offsets(key, part):
    key = jax.random.fold_in(key, 7)
    dilation_rates = jnp.array([DILATION_TWO, DILATION_THREE, DILATION_FOUR], jnp.int32)
    drawn = jax.random.randint(jax.random.fold_in(key, 1), (3, HEAD_TOTAL), 0, dilation_rates[:, None])
    ordering = jax.vmap(lambda subkey: jax.random.permutation(subkey, HEAD_TOTAL))(jax.random.split(jax.random.fold_in(key, 2), 3))
    column = jnp.arange(HEAD_TOTAL, dtype=jnp.int32)[None, :]
    drawn = jnp.where(column == ordering[:, 0:1], 0, drawn)
    drawn = jnp.where(column == ordering[:, 1:2], dilation_rates[:, None] - 1, drawn)
    return drawn.astype(jnp.int32)


def draw_queries(key, part):
    key = jax.random.fold_in(key, 3)
    values = jnp.clip(jax.random.normal(key, (SEQ, D), jnp.float32), -4.0, 4.0)
    return values.astype(jnp.bfloat16)


def draw_key_states(key, part):
    key = jax.random.fold_in(key, 5)
    values = jnp.clip(jax.random.normal(key, (SEQ, D), jnp.float32), -4.0, 4.0)
    return values.astype(jnp.bfloat16)


def block_levels(own_key, dims, cuts, smallest, top_value):
    gain, own = 1.0, jax.random.fold_in(own_key, 6)
    for position, parts in cuts:
        draws = jnp.exp(jax.random.uniform(jax.random.fold_in(own, position), (parts,), jnp.float32, smallest / len(cuts), top_value / len(cuts)))
        gain = gain * jnp.repeat(draws, dims[position] // parts).reshape([-1 if axis == position else 1 for axis in range(len(dims))])
    return gain


def scatter_about(stream_key, extent, scale, most, cuts=(), kind=jnp.bfloat16):
    result = scale * jax.random.normal(stream_key, extent, jnp.float32)
    if cuts:
        result = result * block_levels(stream_key, extent, cuts, -0.22, 0.18)
    return jnp.clip(result, -most, most).astype(kind)


def setup_inputs(seed: int = 0) -> dict:
    key_list = jax.random.split(jax.random.key(seed), 6)
    return {
        "queries": draw_queries(jax.random.fold_in(key_list[5], 71), 0),
        "key_states": draw_key_states(jax.random.fold_in(key_list[5], 71), 0),
        "value_states": scatter_about(key_list[2], (SEQ, D), 1.0, 6.0, ((0, 256),)),
        "cotangent": scatter_about(key_list[3], (SEQ, D), 1.0, 6.0, ((0, 256),)),
        "offsets": draw_offsets(jax.random.fold_in(key_list[5], 71), 0),
    }


def pick_rows(tensor, offset_row, dilation):
    selected = tensor.shape[0] // dilation
    shaped = tensor.reshape(selected, dilation, tensor.shape[1], tensor.shape[2])
    chosen = jnp.arange(dilation, dtype=jnp.int32)[:, None] == offset_row[None, :].astype(jnp.int32)
    return jnp.sum(jnp.where(chosen[None, :, :, None], shaped, jnp.zeros((), tensor.dtype)), axis=1)


def place_rows(tensor, offset_row, dilation):
    chosen = jnp.arange(dilation, dtype=jnp.int32)[:, None] == offset_row[None, :].astype(jnp.int32)
    spread = jnp.where(chosen[None, :, :, None], tensor[:, None], jnp.zeros((), tensor.dtype))
    return spread.reshape(tensor.shape[0] * dilation, tensor.shape[1], tensor.shape[2])


def forward_core(query_rows, key_rows, value_rows):
    factor = query_rows.shape[-1] ** -0.5
    scores = jnp.einsum("qhc,khc->hqk", query_rows.astype(jnp.float32), key_rows.astype(jnp.float32)) * factor
    weights = jnp.exp(scores)
    sums_row = jnp.sum(weights, axis=-1)
    rounded = (weights / sums_row[:, :, None]).astype(jnp.bfloat16)
    output = jnp.einsum("hqk,khc->qhc", rounded.astype(jnp.float32), value_rows.astype(jnp.float32))
    return output, sums_row.T


def backward_core(query_rows, key_rows, value_rows, grad_rows, totals, row_dots):
    factor = query_rows.shape[-1] ** -0.5
    scores = jnp.einsum("qhc,khc->hqk", query_rows.astype(jnp.float32), key_rows.astype(jnp.float32)) * factor
    shares = jnp.exp(scores) / totals.T[:, :, None]
    rounded = shares.astype(jnp.bfloat16)
    grad_probs = jnp.einsum("qhc,khc->hqk", grad_rows.astype(jnp.float32), value_rows.astype(jnp.float32))
    grad_scores = (shares * (grad_probs - row_dots.T[:, :, None])).astype(jnp.bfloat16).astype(jnp.float32)
    query_part = jnp.einsum("hqk,khc->qhc", grad_scores, key_rows.astype(jnp.float32)) * factor
    key_part = jnp.einsum("hqk,qhc->khc", grad_scores, query_rows.astype(jnp.float32)) * factor
    value_part = jnp.einsum("hqk,qhc->khc", rounded.astype(jnp.float32), grad_rows.astype(jnp.float32))
    return query_part, key_part, value_part


def reference(queries, key_states, value_states, cotangent, offsets):
    length, model_width = queries.shape
    head_size = model_width // HEAD_TOTAL

    def split_heads(tensor):
        return tensor.reshape(length, HEAD_TOTAL, head_size)

    query_heads = split_heads(queries)
    key_heads = split_heads(key_states)
    value_heads = split_heads(value_states)
    grad_heads = split_heads(cotangent)
    branch_list = [(1, jnp.zeros((HEAD_TOTAL,), jnp.int32), SEGMENT_ONE), (DILATION_TWO, offsets[0], SEGMENT_TWO), (DILATION_THREE, offsets[1], SEGMENT_THREE), (DILATION_FOUR, offsets[2], SEGMENT_FOUR)]
    numerator = jnp.zeros((length, HEAD_TOTAL, head_size), jnp.float32)
    totals = jnp.zeros((length, HEAD_TOTAL, 1), jnp.float32)
    for dilation, offset_row, span in branch_list:
        per_segment = span // dilation

        def segments(tensor):
            picked = pick_rows(tensor, offset_row, dilation)
            return picked.reshape(length // span, per_segment, HEAD_TOTAL, picked.shape[2])

        output, sums_row = lax.map(lambda blocks: forward_core(*blocks), (segments(query_heads), segments(key_heads), segments(value_heads)))
        output = output.reshape(length // dilation, HEAD_TOTAL, head_size)
        sums_row = sums_row.reshape(length // dilation, HEAD_TOTAL, 1)
        numerator = numerator + place_rows(output * sums_row, offset_row, dilation)
        totals = totals + place_rows(sums_row, offset_row, dilation)
    merged = numerator / totals
    attended = merged.astype(jnp.bfloat16).reshape(length, model_width)
    row_dots = jnp.sum(grad_heads.astype(jnp.float32) * merged, axis=-1, keepdims=True)
    grad_query = jnp.zeros((length, HEAD_TOTAL, head_size), jnp.float32)
    grad_keys = jnp.zeros((length, HEAD_TOTAL, head_size), jnp.float32)
    grad_values = jnp.zeros((length, HEAD_TOTAL, head_size), jnp.float32)
    for dilation, offset_row, span in branch_list:
        per_segment = span // dilation

        def segments(tensor):
            picked = pick_rows(tensor, offset_row, dilation)
            return picked.reshape(length // span, per_segment, HEAD_TOTAL, picked.shape[2])

        parts_out = lax.map(lambda blocks: backward_core(*blocks), (segments(query_heads), segments(key_heads), segments(value_heads), segments(grad_heads), segments(totals)[..., 0], segments(row_dots)[..., 0]))
        query_part, key_part, value_part = [part.reshape(length // dilation, HEAD_TOTAL, head_size) for part in parts_out]
        grad_query = grad_query + place_rows(query_part, offset_row, dilation)
        grad_keys = grad_keys + place_rows(key_part, offset_row, dilation)
        grad_values = grad_values + place_rows(value_part, offset_row, dilation)
    return (attended,
            grad_query.astype(jnp.bfloat16).reshape(length, model_width),
            grad_keys.astype(jnp.bfloat16).reshape(length, model_width),
            grad_values.astype(jnp.bfloat16).reshape(length, model_width))
```

```python
import math

import jax
import jax.numpy as jnp
from jax import lax
from jax.experimental import pallas as pl
from jax.experimental.pallas import tpu as pltpu
from jax.sharding import Mesh, PartitionSpec as P

HEADS = 16
WIDTH = 48
ROWS = 256
GROUP = 16
GROUP_ROWS = GROUP * ROWS
STRIDES = (8, 64, 256)
PICK_TWO = GROUP_ROWS // 8
PICK_THREE = GROUP_ROWS // 64
PICK_FOUR = GROUP_ROWS // 256
PICK_FAR = PICK_THREE + PICK_FOUR
FACTOR = WIDTH**-0.5
EXPONENT = FACTOR * math.log2(math.e)
BF16 = jnp.bfloat16
F32 = jnp.float32
LIMIT = 56 * 1024 * 1024

INSIDE = ("z_low", "x", "core")
ACROSS = ("y", "z_high")


def dot(a, b):
    return lax.dot_general(a, b, (((1,), (0,)), ((), ())), preferred_element_type=F32)


def dot_t(a, b):
    return lax.dot_general(a, b, (((1,), (1,)), ((), ())), preferred_element_type=F32)


def call(kernel, out_shape, scratch=(), smem=0, args=()):
    vmem = pl.BlockSpec(memory_space=pltpu.VMEM)
    specs = [pl.BlockSpec(memory_space=pltpu.SMEM)] * smem + [vmem] * (len(args) - smem)
    return pl.pallas_call(
        kernel,
        out_shape=out_shape,
        in_specs=specs,
        out_specs=jax.tree.map(lambda _: vmem, out_shape),
        scratch_shapes=list(scratch),
        compiler_params=pltpu.CompilerParams(vmem_limit_bytes=LIMIT),
    )(*args)


def pack_kernel(k_ref, v_ref, q_ref, g_ref, out_ref):
    for place, ref in enumerate((k_ref, v_ref, q_ref, g_ref)):
        turned = ref[...].T
        out_ref[:, place * WIDTH : (place + 1) * WIDTH, :] = turned.reshape(HEADS, WIDTH, ROWS)


def unpack_kernel(in_ref, a_ref, q_ref, k_ref, v_ref):
    for place, ref in enumerate((a_ref, q_ref, k_ref, v_ref)):
        block = in_ref[:, place * WIDTH : (place + 1) * WIDTH, :].reshape(HEADS * WIDTH, ROWS)
        ref[...] = block.T


def select_kernel(off_ref, r_ref, kv2_ref, qg2_ref, kv_far_ref, qg_far_ref):
    o2, o3, o4 = off_ref[0], off_ref[1], off_ref[2]
    count = ROWS // 8
    row = lax.broadcasted_iota(jnp.int32, (count + PICK_FAR, ROWS), 0)
    col = lax.broadcasted_iota(jnp.int32, (count + PICK_FAR, ROWS), 1)
    three = row - count
    four = three - PICK_THREE
    near = row < count
    is_three = jnp.logical_and(three >= 0, four < 0)
    target = jnp.where(near, 8 * row + o2, jnp.where(is_three, 64 * (three & 3) + o3, o4))
    source = jnp.where(is_three, three >> 2, four)
    hit = col == target
    far_kv = jnp.zeros((PICK_FAR, 2 * WIDTH), F32)
    far_qg = jnp.zeros((PICK_FAR, 2 * WIDTH), F32)
    for s in range(GROUP):
        chosen = jnp.logical_and(hit, jnp.logical_or(near, source == s))
        chosen = jnp.where(chosen, 1.0, 0.0).astype(BF16)
        kv = dot_t(chosen, r_ref[s, : 2 * WIDTH, :])
        qg = dot_t(chosen, r_ref[s, 2 * WIDTH :, :])
        kv2_ref[s * count : (s + 1) * count, :] = kv[:count].astype(BF16)
        qg2_ref[s * count : (s + 1) * count, :] = qg[:count].astype(BF16)
        far_kv = far_kv + kv[count:]
        far_qg = far_qg + qg[count:]
    qg_far_ref[...] = far_qg.astype(BF16)
    low = far_kv.astype(BF16)
    for s in range(GROUP):
        kv_far_ref[s] = low


def upper(q_t):
    return jnp.concatenate([q_t, jnp.zeros_like(q_t)], axis=0)


def lower(g_t):
    return jnp.concatenate([jnp.zeros_like(g_t), g_t], axis=0)


def forward_unit(kv, v_t, q_t):
    weights = jnp.exp2(dot(kv, upper(q_t)) * EXPONENT)
    sums = jnp.sum(weights, axis=0, keepdims=True)
    low = (weights * (1.0 / (sums * 0.25))).astype(BF16)
    output = dot(v_t, low) * 0.25
    return output * sums, sums


def to_rows(numerator, sums):
    queries = numerator.shape[1]
    block = jnp.concatenate(
        [numerator, jnp.broadcast_to(sums, (80, queries))], axis=0
    )
    return block.T


def backward_unit(kv, q_t, g_t, inverse, dots):
    shares = jnp.exp2(dot(kv, upper(q_t)) * EXPONENT) * inverse
    probs = dot(kv, lower(g_t))
    grad = (shares * (probs - dots)).astype(BF16)
    return shares.astype(BF16), grad


def turn(x):
    return x.T


def stack_far(all_ref, half):
    base = half * 8
    three = jnp.concatenate([all_ref[base + j, :PICK_THREE, :] for j in range(8)], axis=0)
    four = jnp.concatenate([all_ref[j, PICK_THREE:, :] for j in range(16)], axis=0)
    return three, four


def forward_kernel(
    off_ref, r_ref, kv2_ref, qg2_ref, kv_all_ref, qg_far_ref,
    att_ref, td_ref, td2_ref, far_ref, acc_ref, tdr_ref,
):
    o2, o3, o4, half = off_ref[0], off_ref[1], off_ref[2], off_ref[3]

    def segment(seg, carry):
        kv_t = jnp.concatenate([r_ref[2 * seg, : 2 * WIDTH, :], r_ref[2 * seg + 1, : 2 * WIDTH, :]], axis=1)
        kv = turn(kv_t)
        for part in range(2):
            s = 2 * seg + part
            numerator, sums = forward_unit(kv, kv_t[WIDTH:], r_ref[s, 2 * WIDTH : 3 * WIDTH, :])
            acc_ref[pl.ds(pl.multiple_of(s * ROWS, ROWS), ROWS), :] = to_rows(numerator, sums)
        return carry

    lax.fori_loop(0, 8, segment, 0)

    kv2 = kv2_ref[...]
    kv2_t = turn(kv2)
    qg2_t = turn(qg2_ref[...])
    for part in range(2):
        span = slice(part * 256, part * 256 + 256)
        numerator, sums = forward_unit(kv2, kv2_t[WIDTH:], qg2_t[:WIDTH, span])
        rows = pl.ds(part * 2048 + o2, 256, stride=8)
        acc_ref[rows, :] = acc_ref[rows, :] + to_rows(numerator, sums)

    kv3, kv4 = stack_far(kv_all_ref, half)
    qg_far = qg_far_ref[...]
    qg_far_t = turn(jnp.concatenate([qg_far, jnp.zeros((128 - PICK_FAR, 2 * WIDTH), BF16)], axis=0))
    q_far_t = qg_far_t[:WIDTH]
    numerator, sums = forward_unit(kv3, turn(kv3)[WIDTH:], q_far_t)
    rows = pl.ds(o3, PICK_THREE, stride=64)
    acc_ref[rows, :] = acc_ref[rows, :] + to_rows(numerator, sums)[:PICK_THREE]
    numerator, sums = forward_unit(kv4, turn(kv4)[WIDTH:], q_far_t)
    rows = pl.ds(o4, PICK_FOUR, stride=256)
    acc_ref[rows, :] = acc_ref[rows, :] + to_rows(numerator, sums)[PICK_THREE:PICK_FAR]

    def finish(s, carry):
        rows = pl.ds(pl.multiple_of(s * ROWS, ROWS), ROWS)
        block = acc_ref[rows, :].T
        total = block[WIDTH : WIDTH + 1]
        merged = block[:WIDTH] / total
        att_ref[s] = merged.astype(BF16)
        dots = jnp.sum(r_ref[s, 3 * WIDTH :, :].astype(F32) * merged, axis=0, keepdims=True)
        inverse = 1.0 / (total * 0.25)
        both = jnp.concatenate(
            [inverse, dots, jnp.zeros((126, ROWS), F32)], axis=0
        )
        td_ref[s] = both[:8]
        tdr_ref[rows, :] = both.T
        return carry

    lax.fori_loop(0, GROUP, finish, 0)

    td2_ref[...] = tdr_ref[pl.ds(o2, PICK_TWO, stride=8), :].T[:8]
    three = tdr_ref[pl.ds(o3, PICK_THREE, stride=64), :]
    four = tdr_ref[pl.ds(o4, PICK_FOUR, stride=256), :]
    td_far = jnp.concatenate([three, four], axis=0)
    block = jnp.concatenate([qg_far.astype(F32), td_far[:, : 128 - 2 * WIDTH]], axis=1)
    for s in range(GROUP):
        far_ref[s] = block


def backward_kernel(
    off_ref, r_ref, kv2_ref, qg2_ref, kv_all_ref, qg_all_ref, kv_far_ref, own_far_ref, att_ref, td_ref, td2_ref,
    out_ref, accq_ref, acckv_ref,
):
    o2, o3, o4, half = off_ref[0], off_ref[1], off_ref[2], off_ref[3]
    scale = FACTOR * 0.25

    def pick(grad_part, value_part):
        lane = lax.broadcasted_iota(jnp.int32, grad_part.shape, 1)
        return jnp.where(lane < WIDTH, grad_part * scale, value_part * 0.25)

    def widen(x):
        return jnp.concatenate([x, jnp.zeros((x.shape[0], 128 - x.shape[1]), F32)], axis=1)

    def query_rows(part_t):
        return jnp.concatenate([part_t * scale, jnp.zeros((128 - WIDTH, part_t.shape[1]), F32)], axis=0).T

    def segment(seg, carry):
        kv_t = jnp.concatenate([r_ref[2 * seg, : 2 * WIDTH, :], r_ref[2 * seg + 1, : 2 * WIDTH, :]], axis=1)
        kv = turn(kv_t)
        total_grad = jnp.zeros((512, 2 * WIDTH), F32)
        total_value = jnp.zeros((512, 2 * WIDTH), F32)
        for part in range(2):
            s = 2 * seg + part
            qg_t = r_ref[s, 2 * WIDTH :, :]
            shares, grad = backward_unit(
                kv, qg_t[:WIDTH], qg_t[WIDTH:], td_ref[s, 0:1, :], td_ref[s, 1:2, :]
            )
            accq_ref[pl.ds(pl.multiple_of(s * ROWS, ROWS), ROWS), :] = query_rows(dot(kv_t[:WIDTH], grad))
            qg = turn(qg_t)
            total_grad = total_grad + dot(grad, qg)
            total_value = total_value + dot(shares, qg)
        acckv_ref[pl.ds(pl.multiple_of(seg * 512, 512), 512), :] = widen(pick(total_grad, total_value))
        return carry

    lax.fori_loop(0, 8, segment, 0)

    kv2 = kv2_ref[...]
    kv2_t = turn(kv2)
    qg2 = qg2_ref[...]
    qg2_t = turn(qg2)
    total_grad = jnp.zeros((512, 2 * WIDTH), F32)
    total_value = jnp.zeros((512, 2 * WIDTH), F32)
    for part in range(2):
        span = slice(part * 256, part * 256 + 256)
        shares, grad = backward_unit(
            kv2, qg2_t[:WIDTH, span], qg2_t[WIDTH:, span], td2_ref[0:1, span], td2_ref[1:2, span]
        )
        rows = pl.ds(part * 2048 + o2, 256, stride=8)
        accq_ref[rows, :] = accq_ref[rows, :] + query_rows(dot(kv2_t[:WIDTH], grad))
        total_grad = total_grad + dot(grad, qg2[span])
        total_value = total_value + dot(shares, qg2[span])
    rows = pl.ds(o2, PICK_TWO, stride=8)
    acckv_ref[rows, :] = acckv_ref[rows, :] + widen(pick(total_grad, total_value))

    kv3, kv4 = stack_far(kv_all_ref, half)
    far3, far4 = stack_far(qg_all_ref, half)
    own_t = jnp.concatenate([own_far_ref[0], jnp.zeros((128 - PICK_FAR, 128), F32)], axis=0).T
    kv_own = kv_far_ref[0]
    for kv, far, stride, offset, low, count in (
        (kv3, far3, 64, o3, 0, PICK_THREE),
        (kv4, far4, 256, o4, PICK_THREE, PICK_FOUR),
    ):
        rows = pl.ds(offset, count, stride=stride)
        shares, grad = backward_unit(
            kv, own_t[:WIDTH].astype(BF16), own_t[WIDTH : 2 * WIDTH].astype(BF16),
            own_t[2 * WIDTH : 2 * WIDTH + 1], own_t[2 * WIDTH + 1 : 2 * WIDTH + 2],
        )
        part = query_rows(dot(turn(kv)[:WIDTH], grad))
        accq_ref[rows, :] = accq_ref[rows, :] + part[low : low + count]
        far_t = far.T
        qg = far[:, : 2 * WIDTH].astype(BF16)
        shares, grad = backward_unit(
            kv_own, far_t[:WIDTH].astype(BF16), far_t[WIDTH : 2 * WIDTH].astype(BF16),
            far_t[2 * WIDTH : 2 * WIDTH + 1], far_t[2 * WIDTH + 1 : 2 * WIDTH + 2],
        )
        part = widen(pick(dot(grad, qg), dot(shares, qg)))
        acckv_ref[rows, :] = acckv_ref[rows, :] + part[low : low + count]

    def finish(s, carry):
        rows = pl.ds(pl.multiple_of(s * ROWS, ROWS), ROWS)
        out_ref[s, :WIDTH, :] = att_ref[s]
        out_ref[s, WIDTH : 2 * WIDTH, :] = accq_ref[rows, :].T[:WIDTH].astype(BF16)
        out_ref[s, 2 * WIDTH :, :] = acckv_ref[rows, :].T[: 2 * WIDTH].astype(BF16)
        return carry

    lax.fori_loop(0, GROUP, finish, 0)


def per_device(queries, key_states, value_states, cotangent, offsets):
    struct = jax.ShapeDtypeStruct
    head = lax.axis_index(INSIDE)
    across = lax.axis_index(ACROSS)
    own = lax.dynamic_slice(offsets, (0, head), (3, 1))[:, 0]
    scalars = jnp.concatenate([own, (across // 8).astype(jnp.int32)[None]])

    packed = call(
        pack_kernel, struct((HEADS, 4 * WIDTH, ROWS), BF16), args=(key_states, value_states, queries, cotangent)
    )
    r = lax.all_to_all(packed, INSIDE, 0, 0, tiled=True)
    kv2, qg2, kv_far, qg_far = call(
        select_kernel,
        (
            struct((PICK_TWO, 2 * WIDTH), BF16),
            struct((PICK_TWO, 2 * WIDTH), BF16),
            struct((GROUP, PICK_FAR, 2 * WIDTH), BF16),
            struct((PICK_FAR, 2 * WIDTH), BF16),
        ),
        smem=1,
        args=(scalars, r),
    )
    kv_all = lax.all_to_all(kv_far, ACROSS, 0, 0, tiled=True)
    att, td, td2, far = call(
        forward_kernel,
        (
            struct((GROUP, WIDTH, ROWS), BF16),
            struct((GROUP, 8, ROWS), F32),
            struct((8, PICK_TWO), F32),
            struct((GROUP, PICK_FAR, 128), F32),
        ),
        scratch=(pltpu.VMEM((GROUP_ROWS, 128), F32), pltpu.VMEM((GROUP_ROWS, 128), F32)),
        smem=1,
        args=(scalars, r, kv2, qg2, kv_all, qg_far),
    )
    qg_all = lax.all_to_all(far, ACROSS, 0, 0, tiled=True)
    back = call(
        backward_kernel,
        struct((GROUP, 4 * WIDTH, ROWS), BF16),
        scratch=(pltpu.VMEM((GROUP_ROWS, 128), F32), pltpu.VMEM((GROUP_ROWS, 128), F32)),
        smem=1,
        args=(scalars, r, kv2, qg2, kv_all, qg_all, kv_far, far, att, td, td2),
    )
    out = lax.all_to_all(back, INSIDE, 0, 0, tiled=True)
    shape = struct((ROWS, HEADS * WIDTH), BF16)
    return tuple(call(unpack_kernel, (shape,) * 4, args=(out,)))


def solution(mesh):
    axes = ("y", "z_high", "z_low", "x", "core")
    inner = Mesh(mesh.devices.reshape(4, 4, 2, 4, 2), axes)
    rows = P(axes, None)
    return jax.shard_map(
        per_device,
        mesh=inner,
        in_specs=(rows, rows, rows, rows, P()),
        out_specs=(rows, rows, rows, rows),
        check_vma=False,
    )
```

```python
import math

import jax
import jax.numpy as jnp
from jax import lax
from jax.experimental import pallas as pl
from jax.experimental.pallas import tpu as pltpu
from jax.sharding import Mesh, PartitionSpec as P

HEADS = 16
WIDTH = 48
ROWS = 256
GROUP = 16
GROUP_ROWS = GROUP * ROWS
STRIDES = (8, 64, 256)
PICK_TWO = GROUP_ROWS // 8
PICK_THREE = GROUP_ROWS // 64
PICK_FOUR = GROUP_ROWS // 256
PICK_FAR = PICK_THREE + PICK_FOUR
FACTOR = WIDTH**-0.5
EXPONENT = FACTOR * math.log2(math.e)
BF16 = jnp.bfloat16
F32 = jnp.float32
LIMIT = 56 * 1024 * 1024

INSIDE = ("z_low", "x", "core")
ACROSS = ("y", "z_high")


def dot(a, b):
    return lax.dot_general(a, b, (((1,), (0,)), ((), ())), preferred_element_type=F32)


def dot_t(a, b):
    return lax.dot_general(a, b, (((1,), (1,)), ((), ())), preferred_element_type=F32)


def call(kernel, out_shape, scratch=(), smem=0, args=()):
    vmem = pl.BlockSpec(memory_space=pltpu.VMEM)
    specs = [pl.BlockSpec(memory_space=pltpu.SMEM)] * smem + [vmem] * (len(args) - smem)
    return pl.pallas_call(
        kernel,
        out_shape=out_shape,
        in_specs=specs,
        out_specs=jax.tree.map(lambda _: vmem, out_shape),
        scratch_shapes=list(scratch),
        compiler_params=pltpu.CompilerParams(vmem_limit_bytes=LIMIT),
    )(*args)


def pack_kernel(k_ref, v_ref, q_ref, g_ref, out_ref):
    for place, ref in enumerate((k_ref, v_ref, q_ref, g_ref)):
        turned = ref[...].T
        out_ref[:, place * WIDTH : (place + 1) * WIDTH, :] = turned.reshape(HEADS, WIDTH, ROWS)


def unpack_kernel(in_ref, a_ref, q_ref, k_ref, v_ref):
    for place, ref in enumerate((a_ref, q_ref, k_ref, v_ref)):
        block = in_ref[:, place * WIDTH : (place + 1) * WIDTH, :].reshape(HEADS * WIDTH, ROWS)
        ref[...] = block.T


def far_choice(o3, o4, s):
    row = lax.broadcasted_iota(jnp.int32, (PICK_FAR, ROWS), 0)
    col = lax.broadcasted_iota(jnp.int32, (PICK_FAR, ROWS), 1)
    four = row - PICK_THREE
    is_three = four < 0
    target = jnp.where(is_three, 64 * (row & 3) + o3, o4)
    source = jnp.where(is_three, row >> 2, four)
    hit = jnp.logical_and(col == target, source == s)
    return jnp.where(hit, 1.0, 0.0).astype(BF16)


def two_choice(o2):
    row = lax.broadcasted_iota(jnp.int32, (ROWS // 8, ROWS), 0)
    col = lax.broadcasted_iota(jnp.int32, (ROWS // 8, ROWS), 1)
    return jnp.where(col == 8 * row + o2, 1.0, 0.0).astype(BF16)


def upper(q_t):
    return jnp.concatenate([q_t, jnp.zeros_like(q_t)], axis=0)


def lower(g_t):
    return jnp.concatenate([jnp.zeros_like(g_t), g_t], axis=0)


def forward_units(blocks):
    scores = [dot(kv, upper(q_t)) for kv, _, q_t in blocks]
    weights = [jnp.exp2(score * EXPONENT) for score in scores]
    sums = [jnp.sum(weight, axis=0, keepdims=True) for weight in weights]
    low = [(weight * (1.0 / (total * 0.25))).astype(BF16) for weight, total in zip(weights, sums)]
    outputs = [dot(block[1], probs) * 0.25 for block, probs in zip(blocks, low)]
    return [(output * total, total) for output, total in zip(outputs, sums)]


def forward_unit(kv, v_t, q_t):
    return forward_units([(kv, v_t, q_t)])[0]


def to_rows(numerator, sums):
    queries = numerator.shape[1]
    block = jnp.concatenate(
        [numerator, jnp.broadcast_to(sums, (80, queries))], axis=0
    )
    return block.T


def backward_units(blocks):
    scores = [dot(block[0], upper(block[1])) for block in blocks]
    probs = [dot(block[0], lower(block[2])) for block in blocks]
    shares = [jnp.exp2(score * EXPONENT) * block[3] for score, block in zip(scores, blocks)]
    grads = [(share * (prob - block[4])).astype(BF16) for share, prob, block in zip(shares, probs, blocks)]
    return [(share.astype(BF16), grad) for share, grad in zip(shares, grads)]


def backward_unit(kv, q_t, g_t, inverse, dots):
    return backward_units([(kv, q_t, g_t, inverse, dots)])[0]


def pair(ref, seg, low, high):
    return jnp.concatenate([ref[2 * seg, low:high, :], ref[2 * seg + 1, low:high, :]], axis=1)


def turn(x):
    return x.T


FAR_LANES = 256
TD = 4 * WIDTH


def thirds(x):
    high = x.astype(BF16).astype(F32)
    rest = x - high
    middle = rest.astype(BF16).astype(F32)
    return high, middle, rest - middle


def near_forward_kernel(off_ref, r_ref, acc_ref, kv2_ref, qg2_ref, far_ref):
    o2, o3, o4 = off_ref[0], off_ref[1], off_ref[2]
    count = ROWS // 8
    two = two_choice(o2)
    for s in range(GROUP):
        kv2_ref[s * count : (s + 1) * count, :] = dot_t(two, r_ref[s, : 2 * WIDTH, :]).astype(BF16)
        qg2_ref[s * count : (s + 1) * count, :] = dot_t(two, r_ref[s, 2 * WIDTH :, :]).astype(BF16)
    picked = jnp.zeros((PICK_FAR, 4 * WIDTH), F32)
    for s in range(GROUP):
        picked = picked + dot_t(far_choice(o3, o4, s), r_ref[s])

    def segments(step, carry):
        blocks = []
        for j in range(4):
            seg = 4 * step + j
            kv_t = pair(r_ref, seg, 0, 2 * WIDTH)
            blocks.append((turn(kv_t), kv_t[WIDTH:], pair(r_ref, seg, 2 * WIDTH, 3 * WIDTH)))
        for j, (numerator, sums) in enumerate(forward_units(blocks)):
            start = pl.multiple_of((4 * step + j) * 512, 512)
            acc_ref[pl.ds(start, 512), :] = to_rows(numerator, sums)
        return carry

    lax.fori_loop(0, 2, segments, 0)

    kv2 = kv2_ref[...]
    numerator, sums = forward_unit(kv2, turn(kv2)[WIDTH:], turn(qg2_ref[...])[:WIDTH])
    rows = pl.ds(o2, PICK_TWO, stride=8)
    acc_ref[rows, :] = acc_ref[rows, :] + to_rows(numerator, sums)

    base = jnp.concatenate(
        [acc_ref[pl.ds(o3, PICK_THREE, stride=64), :], acc_ref[pl.ds(o4, PICK_FOUR, stride=256), :]], axis=0
    )
    total = base[:, WIDTH : WIDTH + 1]
    merged = base[:, :WIDTH] / total
    dots = jnp.sum(picked[:, 3 * WIDTH :] * merged, axis=1, keepdims=True)
    large, small = total > 2.0**60, total < 2.0**-60
    level = jnp.where(large, 2.0**64, jnp.where(small, 2.0**-64, 1.0))
    unlevel = jnp.where(large, 2.0**-64, jnp.where(small, 2.0**64, 1.0))
    block = jnp.concatenate([picked, jnp.zeros((PICK_FAR, FAR_LANES - TD), F32)], axis=1)
    lane = lax.broadcasted_iota(jnp.int32, block.shape, 1)
    for place, column in enumerate((*thirds(total * unlevel), level, *thirds(dots))):
        block = jnp.where(lane == TD + place, column, block)
    low = block.astype(BF16)
    for s in range(GROUP):
        far_ref[s] = low


def near_sums(far_t):
    td = far_t[TD : TD + 8].astype(F32)
    return (td[0:1] + td[1:2] + td[2:3]) * td[3:4], td[4:5] + td[5:6] + td[6:7]


def pick(grad_part, value_part):
    lane = lax.broadcasted_iota(jnp.int32, grad_part.shape, 1)
    return jnp.where(lane < WIDTH, grad_part * (FACTOR * 0.25), value_part * 0.25)


def widen(x):
    return jnp.concatenate([x, jnp.zeros((x.shape[0], 128 - x.shape[1]), F32)], axis=1)


def query_rows(part_t):
    part_t = part_t * (FACTOR * 0.25)
    return jnp.concatenate([part_t, jnp.zeros((128 - WIDTH, part_t.shape[1]), F32)], axis=0).T


def far_rows(numerator, sums, g_t):
    count = numerator.shape[1]
    lined = jnp.sum(g_t.astype(F32) * numerator, axis=0, keepdims=True)
    block = jnp.concatenate(
        [numerator, jnp.broadcast_to(sums, (8, count)), jnp.broadcast_to(lined, (72, count))], axis=0
    )
    return block.T


def far_units(stacks):
    blocks = []
    turned = []
    for far in stacks:
        far_t = turn(far)
        turned.append(far_t)
        blocks.append((far[:, : 2 * WIDTH], far_t[WIDTH : 2 * WIDTH], far_t[2 * WIDTH : 3 * WIDTH]))
    results = forward_units(blocks)
    return turned, [far_rows(*result, far_t[3 * WIDTH : TD]) for result, far_t in zip(results, turned)]


def totals_of(far_t, rows):
    near_total, near_dots = near_sums(far_t)
    far = rows.T
    total = near_total + far[WIDTH : WIDTH + 1]
    return 1.0 / (total * 0.25), (near_dots * near_total + far[WIDTH + 8 : WIDTH + 9]) / total


def backward_kernel(
    off_ref, r_ref, kv2_ref, qg2_ref, acc_in_ref, all_ref,
    out_ref, acc_ref, td_ref, accq_ref, acckv_ref, three_ref, four_ref,
):
    o2, o3, o4, across = off_ref[0], off_ref[1], off_ref[2], off_ref[3]
    half = across // 8
    meet = (o4 & 63) == o3
    rows2 = pl.ds(o2, PICK_TWO, stride=8)
    rows3 = pl.ds(o3, PICK_THREE, stride=64)
    rows4 = pl.ds(o4, PICK_FOUR, stride=256)
    own_rows3 = pl.ds(pl.multiple_of(across * PICK_THREE, PICK_THREE), PICK_THREE)
    own_rows4 = pl.ds(pl.multiple_of(across * PICK_FOUR, PICK_FOUR), PICK_FOUR)
    half_rows = pl.ds(pl.multiple_of(half * 512, 512), 512)

    acc_ref[...] = acc_in_ref[...]

    def stack_three(which):
        return jnp.concatenate([all_ref[which * 8 + j, :PICK_THREE, :] for j in range(8)], axis=0)

    far3 = stack_three(half)
    far4 = jnp.concatenate([all_ref[j, PICK_THREE:, :] for j in range(GROUP)], axis=0)
    (far3_t, far4_t), (block3, block4) = far_units((far3, far4))
    three_ref[half_rows, :] = block3
    four_ref[...] = block4

    @pl.when(meet)
    def _():
        other = 1 - half
        three_ref[pl.ds(pl.multiple_of(other * 512, 512), 512), :] = far_units((stack_three(other),))[1][0]
        same = pl.ds(o4 >> 6, 256, stride=4)
        both = three_ref[same, :] + four_ref[...]
        three_ref[same, :] = both
        four_ref[...] = both

    acc_ref[rows3, :] = acc_ref[rows3, :] + three_ref[own_rows3, :]
    acc_ref[rows4, :] = acc_ref[rows4, :] + jnp.where(meet, 0.0, four_ref[own_rows4, :])
    inverse3, dots3 = totals_of(far3_t, three_ref[half_rows, :])
    inverse4, dots4 = totals_of(far4_t, four_ref[...])

    def near_totals(block, g_t):
        total = block[WIDTH : WIDTH + 1]
        merged = block[:WIDTH] / total
        dots = jnp.sum(g_t.astype(F32) * merged, axis=0, keepdims=True)
        return merged, 1.0 / (total * 0.25), dots

    def finish(s, carry):
        rows = pl.ds(pl.multiple_of(s * ROWS, ROWS), ROWS)
        merged, inverse, dots = near_totals(acc_ref[rows, :].T, r_ref[s, 3 * WIDTH :, :])
        out_ref[s, :WIDTH, :] = merged.astype(BF16)
        td_ref[s] = jnp.concatenate([inverse, dots, jnp.zeros((6, ROWS), F32)], axis=0)
        return carry

    lax.fori_loop(0, GROUP, finish, 0, unroll=4)

    def segments(step, carry):
        blocks = []
        turned = []
        for j in range(2):
            seg = 2 * step + j
            kv_t = pair(r_ref, seg, 0, 2 * WIDTH)
            qg_t = pair(r_ref, seg, 2 * WIDTH, 4 * WIDTH)
            td = pair(td_ref, seg, 0, 8)
            blocks.append((turn(kv_t), qg_t[:WIDTH], qg_t[WIDTH:], td[0:1], td[1:2]))
            turned.append((kv_t[:WIDTH], turn(qg_t)))
        results = backward_units(blocks)
        query_parts = [dot(keys, grad) for (keys, _), (_, grad) in zip(turned, results)]
        grad_parts = [dot(grad, qg) for (_, qg), (_, grad) in zip(turned, results)]
        value_parts = [dot(share, qg) for (_, qg), (share, _) in zip(turned, results)]
        for j in range(2):
            rows = pl.ds(pl.multiple_of((2 * step + j) * 512, 512), 512)
            accq_ref[rows, :] = query_rows(query_parts[j])
            acckv_ref[rows, :] = widen(pick(grad_parts[j], value_parts[j]))
        return carry

    lax.fori_loop(0, 4, segments, 0)

    qg2 = qg2_ref[...]
    kv2 = kv2_ref[...]
    qg2_t = turn(qg2)
    _, inverse2, dots2 = near_totals(acc_ref[rows2, :].T, qg2_t[WIDTH:])
    own = jnp.concatenate(
        [all_ref[across], jnp.zeros((128 - PICK_FAR, FAR_LANES), BF16)], axis=0
    )
    own_t = turn(own)
    own_block = jnp.concatenate(
        [three_ref[own_rows3, :], four_ref[own_rows4, :], jnp.zeros((128 - PICK_FAR, 128), F32)], axis=0
    )
    own_total, own_lined = near_sums(own_t)
    own_block = own_block.T
    own_lined = own_lined * own_total + own_block[WIDTH + 8 : WIDTH + 9]
    own_total = own_total + own_block[WIDTH : WIDTH + 1]
    own_total = jnp.where(own_total > 0.0, own_total, 1.0)
    own_inverse = 1.0 / (own_total * 0.25)
    own_dots = own_lined / own_total
    own_q, own_g = own_t[2 * WIDTH : 3 * WIDTH], own_t[3 * WIDTH : TD]
    kv_own = own[:, : 2 * WIDTH]
    qg3 = far3[:, 2 * WIDTH : TD]
    qg4 = far4[:, 2 * WIDTH : TD]
    results = backward_units((
        (kv2, qg2_t[:WIDTH], qg2_t[WIDTH:], inverse2, dots2),
        (far3[:, : 2 * WIDTH], own_q, own_g, own_inverse, own_dots),
        (far4[:, : 2 * WIDTH], own_q, own_g, own_inverse, own_dots),
        (kv_own, far3_t[2 * WIDTH : 3 * WIDTH], far3_t[3 * WIDTH : TD], inverse3, dots3),
        (kv_own, far4_t[2 * WIDTH : 3 * WIDTH], far4_t[3 * WIDTH : TD], inverse4, dots4),
    ))
    query2 = query_rows(dot(turn(kv2)[:WIDTH], results[0][1]))
    query3 = query_rows(dot(far3_t[:WIDTH], results[1][1]))
    query4 = query_rows(dot(far4_t[:WIDTH], results[2][1]))
    keys2 = widen(pick(dot(results[0][1], qg2), dot(results[0][0], qg2)))
    keys3 = widen(pick(dot(results[3][1], qg3), dot(results[3][0], qg3)))
    keys4 = widen(pick(dot(results[4][1], qg4), dot(results[4][0], qg4)))
    far_end = PICK_THREE + PICK_FOUR
    for ref, part2, part3, part4 in ((accq_ref, query2, query3, query4), (acckv_ref, keys2, keys3, keys4)):
        ref[rows2, :] = ref[rows2, :] + part2
        ref[rows3, :] = ref[rows3, :] + part3[:PICK_THREE]
        ref[rows4, :] = ref[rows4, :] + part4[PICK_THREE:far_end]

    def leave(s, carry):
        rows = pl.ds(pl.multiple_of(s * ROWS, ROWS), ROWS)
        out_ref[s, WIDTH : 2 * WIDTH, :] = accq_ref[rows, :].astype(BF16).T[:WIDTH]
        out_ref[s, 2 * WIDTH :, :] = acckv_ref[rows, :].astype(BF16).T[: 2 * WIDTH]
        return carry

    lax.fori_loop(0, GROUP, leave, 0, unroll=4)


def per_device(queries, key_states, value_states, cotangent, offsets):
    struct = jax.ShapeDtypeStruct
    head = lax.axis_index(INSIDE)
    across = lax.axis_index(ACROSS)
    own = lax.dynamic_slice(offsets, (0, head), (3, 1))[:, 0]
    scalars = jnp.concatenate([own, across.astype(jnp.int32)[None]])
    scalars, key_states = lax.optimization_barrier((scalars, key_states))

    packed = call(
        pack_kernel, struct((HEADS, 4 * WIDTH, ROWS), BF16), args=(key_states, value_states, queries, cotangent)
    )
    r = lax.all_to_all(packed, INSIDE, 0, 0, tiled=True)
    rows_f32 = struct((GROUP_ROWS, 128), F32)
    scratch = pltpu.VMEM((GROUP_ROWS, 128), F32)
    picked_two = struct((PICK_TWO, 2 * WIDTH), BF16)
    acc, kv2, qg2, far = call(
        near_forward_kernel,
        (rows_f32, picked_two, picked_two, struct((GROUP, PICK_FAR, FAR_LANES), BF16)),
        smem=1,
        args=(scalars, r),
    )
    far_all = lax.all_to_all(far, ACROSS, 0, 0, tiled=True)
    back = call(
        backward_kernel,
        struct((GROUP, 4 * WIDTH, ROWS), BF16),
        scratch=(
            scratch,
            pltpu.VMEM((GROUP, 8, ROWS), F32),
            scratch,
            scratch,
            pltpu.VMEM((1024, 128), F32),
            pltpu.VMEM((256, 128), F32),
        ),
        smem=1,
        args=(scalars, r, kv2, qg2, acc, far_all),
    )
    out = lax.all_to_all(back, INSIDE, 0, 0, tiled=True)
    shape = struct((ROWS, HEADS * WIDTH), BF16)
    return tuple(call(unpack_kernel, (shape,) * 4, args=(out,)))


def solution(mesh):
    axes = ("y", "z_high", "z_low", "x", "core")
    inner = Mesh(mesh.devices.reshape(4, 4, 2, 4, 2), axes)
    rows = P(axes, None)
    return jax.shard_map(
        per_device,
        mesh=inner,
        in_specs=(rows, rows, rows, rows, P()),
        out_specs=(rows, rows, rows, rows),
        check_vma=False,
    )
```

```python
import math

import jax
import jax.numpy as jnp
from jax import lax
from jax.experimental import pallas as pl
from jax.experimental.pallas import tpu as pltpu
from jax.sharding import Mesh, PartitionSpec as P

HEADS = 16
WIDTH = 48
ROWS = 256
OWN = 8
GROUP_ROWS = 16 * ROWS
PICK_TWO = GROUP_ROWS // 8
PICK_THREE = GROUP_ROWS // 64
PICK_FOUR = GROUP_ROWS // 256
PICK_FAR = PICK_THREE + PICK_FOUR
FACTOR = WIDTH**-0.5
EXPONENT = FACTOR * math.log2(math.e)
BF16 = jnp.bfloat16
F32 = jnp.float32
LIMIT = 56 * 1024 * 1024

CHIPS = ("z_low", "x")
HALF = ("y_low", "z_high")


def dot(a, b):
    return lax.dot_general(a, b, (((1,), (0,)), ((), ())), preferred_element_type=F32)


def dot_t(a, b):
    return lax.dot_general(a, b, (((1,), (1,)), ((), ())), preferred_element_type=F32)


def call(kernel, out_shape, scratch=(), smem=0, args=(), steps=0):
    smem_spec = pl.BlockSpec(memory_space=pltpu.SMEM)

    def spec(array):
        if not steps:
            return pl.BlockSpec(memory_space=pltpu.VMEM)
        rest = array.shape[1:]
        return pl.BlockSpec((array.shape[0] // steps, *rest), lambda i: (i,) + (0,) * len(rest))

    return pl.pallas_call(
        kernel,
        out_shape=out_shape,
        grid=(steps,) if steps else (),
        in_specs=[smem_spec] * smem + [spec(array) for array in args[smem:]],
        out_specs=jax.tree.map(spec, out_shape),
        scratch_shapes=list(scratch),
        compiler_params=pltpu.CompilerParams(vmem_limit_bytes=LIMIT),
    )(*args)


def pack_kernel(k_ref, v_ref, q_ref, g_ref, keep_ref, send_ref):
    parts = []
    for ref in (k_ref, v_ref, q_ref, g_ref):
        turned = ref[...].T
        middle = OWN * WIDTH
        parts.append([turned[:middle].reshape(OWN, WIDTH, ROWS), turned[middle:].reshape(OWN, WIDTH, ROWS)])

    def store(low_ref, high_ref):
        for place, (low, high) in enumerate(parts):
            span = slice(place * WIDTH, (place + 1) * WIDTH)
            low_ref[:, span, :] = low
            high_ref[:, span, :] = high

    @pl.when(lax.axis_index("core") == 0)
    def _():
        store(keep_ref, send_ref)

    @pl.when(lax.axis_index("core") == 1)
    def _():
        store(send_ref, keep_ref)


def unpack_kernel(keep_ref, came_ref, a_ref, q_ref, k_ref, v_ref):
    def store(low_ref, high_ref):
        for place, ref in enumerate((a_ref, q_ref, k_ref, v_ref)):
            span = slice(place * WIDTH, (place + 1) * WIDTH)
            low = low_ref[:, span, :].reshape(OWN * WIDTH, ROWS)
            high = high_ref[:, span, :].reshape(OWN * WIDTH, ROWS)
            ref[...] = jnp.concatenate([low, high], axis=0).T

    @pl.when(lax.axis_index("core") == 0)
    def _():
        store(keep_ref, came_ref)

    @pl.when(lax.axis_index("core") == 1)
    def _():
        store(came_ref, keep_ref)


def upper(q_t):
    return jnp.concatenate([q_t, jnp.zeros_like(q_t)], axis=0)


def lower(g_t):
    return jnp.concatenate([jnp.zeros_like(g_t), g_t], axis=0)


def forward_units(blocks):
    scores = [dot(kv, upper(q_t)) for kv, _, q_t in blocks]
    weights = [jnp.exp2(score * EXPONENT) for score in scores]
    sums = [jnp.sum(weight, axis=0, keepdims=True) for weight in weights]
    low = [(weight * (1.0 / (total * 0.25))).astype(BF16) for weight, total in zip(weights, sums)]
    outputs = [dot(block[1], probs) * 0.25 for block, probs in zip(blocks, low)]
    return [(output * total, total) for output, total in zip(outputs, sums)]


def forward_unit(kv, v_t, q_t):
    return forward_units([(kv, v_t, q_t)])[0]


def backward_units(blocks):
    scores = [dot(block[0], upper(block[1])) for block in blocks]
    probs = [dot(block[0], lower(block[2])) for block in blocks]
    shares = [jnp.exp2(score * EXPONENT) * block[3] for score, block in zip(scores, blocks)]
    grads = [(share * (prob - block[4])).astype(BF16) for share, prob, block in zip(shares, probs, blocks)]
    return [(share.astype(BF16), grad) for share, grad in zip(shares, grads)]


def backward_unit(kv, q_t, g_t, inverse, dots):
    return backward_units([(kv, q_t, g_t, inverse, dots)])[0]


def turn(x):
    return x.T


FAR_LANES = 256
TD = 4 * WIDTH
DEN = 96
LINED = 104
TAKEN = 80
SCALE = FACTOR * 0.25


def thirds(x):
    high = x.astype(BF16).astype(F32)
    rest = x - high
    middle = rest.astype(BF16).astype(F32)
    return high, middle, rest - middle


def sum_rows(numerator, sums, g_t):
    count = numerator.shape[1]
    lined = jnp.sum(g_t.astype(F32) * numerator, axis=0, keepdims=True)
    block = jnp.concatenate(
        [
            numerator,
            jnp.zeros((WIDTH, count), F32),
            jnp.broadcast_to(sums, (8, count)),
            jnp.broadcast_to(lined, (24, count)),
        ],
        axis=0,
    )
    return block.T


def query_rows(part_t):
    count = part_t.shape[1]
    return jnp.concatenate([jnp.zeros((WIDTH, count), F32), part_t * SCALE, jnp.zeros((32, count), F32)], axis=0).T


def with_sums(picked, total, dots):
    large, small = total > 2.0**60, total < 2.0**-60
    level = jnp.where(large, 2.0**64, jnp.where(small, 2.0**-64, 1.0))
    unlevel = jnp.where(large, 2.0**-64, jnp.where(small, 2.0**64, 1.0))
    lane = lax.broadcasted_iota(jnp.int32, picked.shape, 1)
    for place, column in enumerate((*thirds(total * unlevel), level, *thirds(dots))):
        picked = jnp.where(lane == TD + place, column, picked)
    return picked.astype(BF16)


def sums_beside(far):
    def column(place):
        return far[:, TD + place : TD + place + 1]

    return (column(0) + column(1) + column(2)) * column(3), column(4) + column(5) + column(6)


def near_sums(far_t):
    td = far_t[TD : TD + 8].astype(F32)
    return (td[0:1] + td[1:2] + td[2:3]) * td[3:4], td[4:5] + td[5:6] + td[6:7]


def pick(grad_part, value_part):
    lane = lax.broadcasted_iota(jnp.int32, grad_part.shape, 1)
    return jnp.where(lane < WIDTH, grad_part * SCALE, value_part * 0.25)


def widen(x):
    return jnp.concatenate([x, jnp.zeros((x.shape[0], 128 - x.shape[1]), F32)], axis=1)


def both(keep_ref, came_ref, j, low, high):
    return jnp.concatenate([keep_ref[j, low:high, :], came_ref[j, low:high, :]], axis=1)


def near_forward_kernel(off_ref, keep_ref, came_ref, acc_ref, taken_ref, base_ref):
    first = OWN * lax.axis_index("core") + 4 * pl.program_id(0)

    blocks = []
    for j in range(4):
        kv_t = both(keep_ref, came_ref, j, 0, 2 * WIDTH)
        blocks.append((turn(kv_t), kv_t[WIDTH:], both(keep_ref, came_ref, j, 2 * WIDTH, 3 * WIDTH)))
    for j, (numerator, sums) in enumerate(forward_units(blocks)):
        g_t = both(keep_ref, came_ref, j, 3 * WIDTH, TD)
        acc_ref[j * 512 : j * 512 + 512, :] = sum_rows(numerator, sums, g_t)

    row = lax.broadcasted_iota(jnp.int32, (TAKEN, 512), 0)
    col = lax.broadcasted_iota(jnp.int32, (TAKEN, 512), 1)
    is_two, is_three = row < 64, row < 72
    start = jnp.where(is_two, 8 * row, jnp.where(is_three, 64 * (row - 64), 256 * (row - 72)))
    for j in range(4):
        o2, o3, o4 = off_ref[0, first + j], off_ref[1, first + j], off_ref[2, first + j]
        base_ref[j, 64:, :] = jnp.ones((16, 128), F32)
        base_ref[j, :64, :] = acc_ref[pl.ds(j * 512 + o2, 64, stride=8), :]
        base_ref[j, 64:72, :] = acc_ref[pl.ds(j * 512 + o3, 8, stride=64), :]
        base_ref[j, 72:74, :] = acc_ref[pl.ds(j * 512 + o4, 2, stride=256), :]
        target = start + jnp.where(is_two, o2, jnp.where(is_three, o3, o4))
        hit = jnp.where(col == target, 1.0, 0.0).astype(BF16)
        picked = dot_t(hit, both(keep_ref, came_ref, j, 0, TD))
        picked = jnp.concatenate([picked, jnp.zeros((TAKEN, FAR_LANES - TD), F32)], axis=1)
        base = base_ref[j]
        total = base[:, DEN : DEN + 1]
        taken_ref[j] = with_sums(picked, total, base[:, LINED : LINED + 1] / total)


def middle_kernel(off_ref, in_ref, block2_ref, far_ref):
    head = OWN * lax.axis_index("core") + lax.axis_index(CHIPS)
    o2, o3, o4 = off_ref[0, head], off_ref[1, head], off_ref[2, head]
    two = jnp.concatenate([in_ref[s, :64, :] for s in range(OWN)], axis=0)
    two_t = turn(two)
    numerator, sums = forward_unit(two[:, : 2 * WIDTH], two_t[WIDTH : 2 * WIDTH], two_t[2 * WIDTH : 3 * WIDTH])
    block2_ref[...] = sum_rows(numerator, sums, two_t[3 * WIDTH : TD])

    rest = jnp.concatenate([in_ref[s, 64:, :] for s in range(OWN)], axis=0)
    row = lax.broadcasted_iota(jnp.int32, (PICK_FAR, 128), 0)
    col = lax.broadcasted_iota(jnp.int32, (PICK_FAR, 128), 1)
    four = row - PICK_THREE
    source = jnp.where(row < PICK_THREE, 16 * (row >> 3) + (row & 7), 16 * (four >> 1) + 8 + (four & 1))
    far = dot(jnp.where(col == source, 1.0, 0.0).astype(BF16), rest)
    total, dots = sums_beside(far)
    from2 = jnp.concatenate(
        [
            jnp.where((o3 & 7) == o2, block2_ref[pl.ds(o3 >> 3, PICK_THREE, stride=8), :], 0.0),
            jnp.where((o4 & 7) == o2, block2_ref[pl.ds(o4 >> 3, PICK_FOUR, stride=32), :], 0.0),
        ],
        axis=0,
    )
    lined = dots * total + from2[:, LINED : LINED + 1]
    total = total + from2[:, DEN : DEN + 1]
    low = with_sums(far, total, lined / total)
    for s in range(8):
        far_ref[s] = low


def far_forward(far):
    far_t = turn(far)
    result = forward_unit(far[:, : 2 * WIDTH], far_t[WIDTH : 2 * WIDTH], far_t[2 * WIDTH : 3 * WIDTH])
    return far_t, sum_rows(*result, far_t[3 * WIDTH : TD])


def three_kernel(off_ref, all_ref, block3_ref, four_ref):
    head = OWN * lax.axis_index("core") + lax.axis_index(CHIPS)
    o3, o4 = off_ref[1, head], off_ref[2, head]
    meet = (o4 & 63) == o3
    far3 = jnp.concatenate([all_ref[j, :PICK_THREE, :] for j in range(8)], axis=0)
    block3_ref[...] = far_forward(far3)[1]
    four = jnp.concatenate([all_ref[j, PICK_THREE:, :] for j in range(8)], axis=0).astype(F32)
    from3 = jnp.where(meet, block3_ref[pl.ds(o4 >> 6, 128, stride=4), :], 0.0)
    total, dots = sums_beside(four)
    lined = dots * total + from3[:, LINED : LINED + 1]
    total = total + from3[:, DEN : DEN + 1]
    four_ref[...] = with_sums(four, total, lined / total)


def totals_of(far_t, rows):
    near_total, near_dots = near_sums(far_t)
    far = rows.T
    total = near_total + far[DEN : DEN + 1]
    total = jnp.where(total > 0.0, total, 1.0)
    return 1.0 / (total * 0.25), (near_dots * near_total + far[LINED : LINED + 1]) / total


def far_kernel(
    off_ref, in_ref, block2_ref, all_ref, block3_ref, here_ref, there_ref,
    out_ref, two_ref, three_ref, four_ref,
):
    head = OWN * lax.axis_index("core") + lax.axis_index(CHIPS)
    group = lax.axis_index(HALF)
    o2, o3, o4 = off_ref[0, head], off_ref[1, head], off_ref[2, head]
    meet = (o4 & 63) == o3
    own_rows3 = pl.ds(pl.multiple_of(group * PICK_THREE, PICK_THREE), PICK_THREE)
    own_rows4 = pl.ds(pl.multiple_of(group * PICK_FOUR, PICK_FOUR), PICK_FOUR)

    far3 = jnp.concatenate([all_ref[j, :PICK_THREE, :] for j in range(8)], axis=0)
    far3_t = turn(far3)
    far4 = jnp.concatenate([here_ref[...], there_ref[...]], axis=0)
    far4_t, block4 = far_forward(far4)
    four_ref[...] = block4
    three_ref[...] = block3_ref[...]
    same = pl.ds(o4 >> 6, 128, stride=4)
    three_ref[same, :] = three_ref[same, :] + jnp.where(meet, four_ref[:128, :], 0.0)

    own3 = three_ref[own_rows3, :]
    own4 = four_ref[own_rows4, :]
    only4 = jnp.where(meet, 0.0, own4)
    two_ref[...] = block2_ref[...]
    in_two = pl.ds(o3 >> 3, PICK_THREE, stride=8)
    two_ref[in_two, :] = two_ref[in_two, :] + jnp.where((o3 & 7) == o2, own3, 0.0)
    in_two = pl.ds(o4 >> 3, PICK_FOUR, stride=32)
    two_ref[in_two, :] = two_ref[in_two, :] + jnp.where((o4 & 7) == o2, only4, 0.0)

    two = jnp.concatenate([in_ref[s, :64, :] for s in range(OWN)], axis=0)
    two_t = turn(two)
    pad = 128 - PICK_FAR
    own = jnp.concatenate(
        [all_ref[group, :PICK_THREE, :], here_ref[own_rows4, :], jnp.zeros((pad, FAR_LANES), BF16)], axis=0
    )
    own_t = turn(own)
    own_block = jnp.concatenate([own3, own4, jnp.zeros((pad, 128), F32)], axis=0)
    inverse2, dots2 = totals_of(two_t, two_ref[...])
    inverse3, dots3 = totals_of(far3_t, three_ref[...])
    inverse4, dots4 = totals_of(far4_t, four_ref[...])
    own_inverse, own_dots = totals_of(own_t, own_block)

    def queries(turned):
        return turned[2 * WIDTH : 3 * WIDTH], turned[3 * WIDTH : TD]

    kv_own = own[:, : 2 * WIDTH]
    results = backward_units((
        (two[:, : 2 * WIDTH], *queries(two_t), inverse2, dots2),
        (far3[:, : 2 * WIDTH], *queries(own_t), own_inverse, own_dots),
        (far4[:, : 2 * WIDTH], *queries(own_t), own_inverse, own_dots),
        (kv_own, *queries(far3_t), inverse3, dots3),
        (kv_own, *queries(far4_t), inverse4, dots4),
    ))
    query2 = query_rows(dot(two_t[:WIDTH], results[0][1])) + block2_ref[...]
    query3 = query_rows(dot(far3_t[:WIDTH], results[1][1]))[:PICK_THREE] + own3
    query4 = query_rows(dot(far4_t[:WIDTH], results[2][1]))[PICK_THREE:PICK_FAR] + only4

    def keys(result, far):
        qg = far[:, 2 * WIDTH : TD]
        return widen(pick(dot(result[1], qg), dot(result[0], qg)))

    keys2 = keys(results[0], two)
    keys3 = keys(results[3], far3)[:PICK_THREE]
    keys4 = keys(results[4], far4)[PICK_THREE:PICK_FAR]
    for lanes, part2, part3, part4 in (
        (slice(0, 128), keys2, keys3, keys4),
        (slice(128, 256), query2, query3, query4),
    ):
        for c in range(OWN):
            out_ref[c, :64, lanes] = part2[64 * c : 64 * c + 64]
            out_ref[c, 64:72, lanes] = part3[8 * c : 8 * c + 8]
            out_ref[c, 72:74, lanes] = part4[2 * c : 2 * c + 2]
            out_ref[c, 74:, lanes] = jnp.zeros((TAKEN - 74, 128), F32)


def near_backward_kernel(
    off_ref, keep_ref, came_ref, acc_ref, back_ref, stay_ref, leave_ref, rows_ref, keys_ref,
):
    first = OWN * lax.axis_index("core") + 2 * pl.program_id(0)

    def add_taken(ref, j, lanes):
        base = j * 512
        for low, high, offset, stride in (
            (0, 64, off_ref[0, first + j], 8),
            (64, 72, off_ref[1, first + j], 64),
            (72, 74, off_ref[2, first + j], 256),
        ):
            rows = pl.ds(base + offset, high - low, stride=stride)
            ref[rows, :] = ref[rows, :] + back_ref[j, low:high, lanes]

    def put(j, low, high, value):
        stay_ref[j, low:high, :] = value[:, :ROWS]
        leave_ref[j, low:high, :] = value[:, ROWS:]

    blocks = []
    turned = []
    rows_ref[...] = acc_ref[...]
    for j in range(2):
        add_taken(rows_ref, j, slice(128, 256))
    for j in range(2):
        kv_t = both(keep_ref, came_ref, j, 0, 2 * WIDTH)
        qg_t = both(keep_ref, came_ref, j, 2 * WIDTH, TD)
        sums = rows_ref[j * 512 : j * 512 + 512, :].T
        total = sums[DEN : DEN + 1]
        merged = sums[:WIDTH] / total
        dots = jnp.sum(qg_t[WIDTH:].astype(F32) * merged, axis=0, keepdims=True)
        put(j, 0, WIDTH, merged.astype(BF16))
        blocks.append((turn(kv_t), qg_t[:WIDTH], qg_t[WIDTH:], 1.0 / (total * 0.25), dots))
        turned.append((kv_t[:WIDTH], turn(qg_t), sums[WIDTH : 2 * WIDTH]))
    results = backward_units(blocks)
    query_parts = [dot(part[0], grad) * SCALE + part[2] for part, (_, grad) in zip(turned, results)]
    grad_parts = [dot(grad, part[1]) for part, (_, grad) in zip(turned, results)]
    value_parts = [dot(share, part[1]) for part, (share, _) in zip(turned, results)]
    for j in range(2):
        put(j, WIDTH, 2 * WIDTH, query_parts[j].astype(BF16))
        keys_ref[j * 512 : j * 512 + 512, :] = widen(pick(grad_parts[j], value_parts[j]))
        add_taken(keys_ref, j, slice(0, 128))
        put(j, 2 * WIDTH, TD, keys_ref[j * 512 : j * 512 + 512, :].astype(BF16).T[: 2 * WIDTH])


def per_device(queries, key_states, value_states, cotangent, offsets):
    struct = jax.ShapeDtypeStruct
    def swap(x):
        return lax.ppermute(x, "core", [(0, 1), (1, 0)])

    half = struct((OWN, 4 * WIDTH, ROWS), BF16)
    keep, send = call(
        pack_kernel, (half, half), args=(key_states, value_states, queries, cotangent)
    )
    came = swap(send)
    rows_f32 = struct((GROUP_ROWS, 128), F32)
    acc, taken = call(
        near_forward_kernel,
        (rows_f32, struct((OWN, TAKEN, FAR_LANES), BF16)),
        scratch=(pltpu.VMEM((4, TAKEN, 128), F32),),
        steps=2,
        smem=1,
        args=(offsets, keep, came),
    )
    taken = lax.all_to_all(taken, CHIPS, 0, 0, tiled=True)
    block2, far = call(
        middle_kernel,
        (struct((PICK_TWO, 128), F32), struct((8, PICK_FAR, FAR_LANES), BF16)),
        smem=1,
        args=(offsets, taken),
    )
    far = lax.all_to_all(far, HALF, 0, 0, tiled=True)
    block3, here = call(
        three_kernel,
        (struct((512, 128), F32), struct((128, FAR_LANES), BF16)),
        smem=1,
        args=(offsets, far),
    )
    there = lax.ppermute(here, "y_high", [(0, 1), (1, 0)])
    back = call(
        far_kernel,
        struct((OWN, TAKEN, 256), F32),
        scratch=(pltpu.VMEM((512, 128), F32), pltpu.VMEM((512, 128), F32), pltpu.VMEM((256, 128), F32)),
        smem=1,
        args=(offsets, taken, block2, far, block3, here, there),
    )
    back = lax.all_to_all(back, CHIPS, 0, 0, tiled=True)
    stay, leave = call(
        near_backward_kernel,
        (half, half),
        scratch=(pltpu.VMEM((1024, 128), F32), pltpu.VMEM((1024, 128), F32)),
        steps=4,
        smem=1,
        args=(offsets, keep, came, acc, back),
    )
    shape = struct((ROWS, HEADS * WIDTH), BF16)
    return tuple(call(unpack_kernel, (shape,) * 4, args=(stay, swap(leave))))


def solution(mesh):
    axes = ("y_high", "y_low", "z_high", "z_low", "x", "core")
    inner = Mesh(mesh.devices.reshape(2, 2, 4, 2, 4, 2), axes)
    rows = P(axes, None)
    return jax.shard_map(
        per_device,
        mesh=inner,
        in_specs=(rows, rows, rows, rows, P()),
        out_specs=(rows, rows, rows, rows),
        check_vma=False,
    )
```

```python
import math

import jax
import jax.numpy as jnp
from jax import lax
from jax.experimental import pallas as pl
from jax.experimental.pallas import tpu as pltpu
from jax.sharding import Mesh, PartitionSpec as P

HEADS = 16
WIDTH = 48
ROWS = 256
HALF_WIDTH = 384
OWN = 8
GROUP_ROWS = 16 * ROWS
PICK_TWO = GROUP_ROWS // 8
PICK_THREE = GROUP_ROWS // 64
PICK_FOUR = GROUP_ROWS // 256
PICK_FAR = PICK_THREE + PICK_FOUR
FACTOR = WIDTH**-0.5
EXPONENT = FACTOR * math.log2(math.e)
BF16 = jnp.bfloat16
F32 = jnp.float32
LIMIT = 32 * 1024 * 1024

CHIPS = ("z_low", "x")
HALF = ("y_low", "z_high")


def dot(a, b):
    return lax.dot_general(a, b, (((1,), (0,)), ((), ())), preferred_element_type=F32)


def dot_t(a, b):
    return lax.dot_general(a, b, (((1,), (1,)), ((), ())), preferred_element_type=F32)


def call(kernel, out_shape, scratch=(), smem=0, args=(), steps=0):
    smem_spec = pl.BlockSpec(memory_space=pltpu.SMEM)

    def spec(array):
        if not steps:
            return pl.BlockSpec(memory_space=pltpu.VMEM)
        rest = array.shape[1:]
        return pl.BlockSpec((array.shape[0] // steps, *rest), lambda i: (i,) + (0,) * len(rest))

    return pl.pallas_call(
        kernel,
        out_shape=out_shape,
        grid=(steps,) if steps else (),
        in_specs=[smem_spec] * smem + [spec(array) for array in args[smem:]],
        out_specs=jax.tree.map(spec, out_shape),
        scratch_shapes=list(scratch),
        compiler_params=pltpu.CompilerParams(vmem_limit_bytes=LIMIT),
    )(*args)


def half_columns(core):
    return pl.ds(pl.multiple_of(core * HALF_WIDTH, HALF_WIDTH), HALF_WIDTH)


def pack_half(arrays, own, half):
    def kernel(k_ref, v_ref, q_ref, g_ref, out_ref, raw_ref, sem_ref):
        core = lax.axis_index("core")
        columns = half_columns(core if own else 1 - core)
        copies = [
            pltpu.make_async_copy(ref.at[:, columns], raw_ref.at[place], sem_ref.at[place])
            for place, ref in enumerate((k_ref, v_ref, q_ref, g_ref))
        ]
        for copy in copies:
            copy.start()
        for place, copy in enumerate(copies):
            copy.wait()
            out_ref[:, place * WIDTH : (place + 1) * WIDTH, :] = raw_ref[place].T.reshape(OWN, WIDTH, ROWS)

    return pl.pallas_call(
        kernel,
        out_shape=half,
        in_specs=[pl.BlockSpec(memory_space=pl.ANY)] * 4,
        out_specs=pl.BlockSpec(memory_space=pltpu.VMEM),
        scratch_shapes=[pltpu.VMEM((4, ROWS, HALF_WIDTH), BF16), pltpu.SemaphoreType.DMA((4,))],
        compiler_params=pltpu.CompilerParams(vmem_limit_bytes=LIMIT),
    )(*arrays)


def unpack_half(half, own, outs):
    shape = pltpu.HBM((ROWS, HEADS * WIDTH), BF16)

    def kernel(in_ref, *refs):
        out_refs, raw_ref, sem_ref = refs[-6:-2], refs[-2], refs[-1]
        core = lax.axis_index("core")
        columns = half_columns(core if own else 1 - core)
        copies = []
        for place, ref in enumerate(out_refs):
            block = in_ref[:, place * WIDTH : (place + 1) * WIDTH, :].reshape(HALF_WIDTH, ROWS)
            raw_ref[place] = block.T
            copy = pltpu.make_async_copy(raw_ref.at[place], ref.at[:, columns], sem_ref.at[place])
            copy.start()
            copies.append(copy)
        for copy in copies:
            copy.wait()

    anywhere = pl.BlockSpec(memory_space=pl.ANY)
    return pl.pallas_call(
        kernel,
        out_shape=(shape,) * 4,
        in_specs=[pl.BlockSpec(memory_space=pltpu.VMEM)] + [anywhere] * len(outs),
        out_specs=(anywhere,) * 4,
        input_output_aliases={place + 1: place for place in range(len(outs))},
        scratch_shapes=[pltpu.VMEM((4, ROWS, HALF_WIDTH), BF16), pltpu.SemaphoreType.DMA((4,))],
        compiler_params=pltpu.CompilerParams(vmem_limit_bytes=LIMIT),
    )(half, *outs)


def upper(q_t):
    return jnp.concatenate([q_t, jnp.zeros_like(q_t)], axis=0)


def lower(g_t):
    return jnp.concatenate([jnp.zeros_like(g_t), g_t], axis=0)


def forward_units(blocks):
    scores = [dot(kv, upper(q_t)) for kv, _, q_t in blocks]
    weights = [jnp.exp2(score * EXPONENT) for score in scores]
    sums = [jnp.sum(weight, axis=0, keepdims=True) for weight in weights]
    low = [(weight * (1.0 / (total * 0.25))).astype(BF16) for weight, total in zip(weights, sums)]
    outputs = [dot(block[1], probs) * 0.25 for block, probs in zip(blocks, low)]
    return [(output * total, total) for output, total in zip(outputs, sums)]


def forward_unit(kv, v_t, q_t):
    middle = q_t.shape[1] // 2
    parts = forward_units([(kv, v_t, q_t[:, :middle]), (kv, v_t, q_t[:, middle:])])
    return tuple(jnp.concatenate(pieces, axis=1) for pieces in zip(*parts))


def backward_units(blocks):
    scores = [dot(block[0], upper(block[1])) for block in blocks]
    probs = [dot(block[0], lower(block[2])) for block in blocks]
    shares = [jnp.exp2(score * EXPONENT) * block[3] for score, block in zip(scores, blocks)]
    grads = [(share * (prob - block[4])).astype(BF16) for share, prob, block in zip(shares, probs, blocks)]
    return [(share.astype(BF16), grad) for share, grad in zip(shares, grads)]


def backward_unit(kv, q_t, g_t, inverse, dots):
    return backward_units([(kv, q_t, g_t, inverse, dots)])[0]


def turn(x):
    return x.T


FAR_LANES = 256
TD = 4 * WIDTH
DEN = 96
LINED = 104
TAKEN = 80
SCALE = FACTOR * 0.25


def thirds(x):
    high = x.astype(BF16).astype(F32)
    rest = x - high
    middle = rest.astype(BF16).astype(F32)
    return high, middle, rest - middle


def sum_columns(numerator, sums, g_t):
    count = numerator.shape[1]
    lined = jnp.sum(g_t.astype(F32) * numerator, axis=0, keepdims=True)
    return jnp.concatenate(
        [
            numerator,
            jnp.zeros((WIDTH, count), F32),
            jnp.broadcast_to(sums, (8, count)),
            jnp.broadcast_to(lined, (24, count)),
        ],
        axis=0,
    )


def sum_rows(numerator, sums, g_t):
    return sum_columns(numerator, sums, g_t).T


def query_rows(part_t):
    count = part_t.shape[1]
    return jnp.concatenate([jnp.zeros((WIDTH, count), F32), part_t * SCALE, jnp.zeros((32, count), F32)], axis=0).T


def with_sums(picked, total, dots):
    large, small = total > 2.0**60, total < 2.0**-60
    level = jnp.where(large, 2.0**64, jnp.where(small, 2.0**-64, 1.0))
    unlevel = jnp.where(large, 2.0**-64, jnp.where(small, 2.0**64, 1.0))
    lane = lax.broadcasted_iota(jnp.int32, picked.shape, 1)
    for place, column in enumerate((*thirds(total * unlevel), level, *thirds(dots))):
        picked = jnp.where(lane == TD + place, column, picked)
    return picked.astype(BF16)


def fold(rows):
    tail = rows[:, 128:]
    pairs = jnp.concatenate([tail[:32, :64], tail[32:64, :64]], axis=1)
    sums = [tail[16 * i : 16 * i + 16, 64:72] for i in range(4)]
    last = jnp.concatenate([tail[64:, :72], *sums, jnp.zeros((16, 24), rows.dtype)], axis=1)
    return jnp.concatenate([rows[:, :128], pairs, last], axis=0)


def unfold(block):
    pairs, last = block[80:112], block[112:]
    tail = jnp.concatenate([pairs[:, :64], pairs[:, 64:]], axis=0)
    sums = jnp.concatenate([last[:, 72 + 8 * i : 80 + 8 * i] for i in range(4)], axis=0)
    three = jnp.concatenate([block[:64], tail, sums, jnp.zeros((64, 56), block.dtype)], axis=1)
    four = jnp.concatenate([block[64:80], last[:, :72], jnp.zeros((16, 56), block.dtype)], axis=1)
    return three, four


def sums_beside(far):
    def column(place):
        return far[:, TD + place : TD + place + 1]

    return (column(0) + column(1) + column(2)) * column(3), column(4) + column(5) + column(6)


def near_sums(far_t):
    td = far_t[TD : TD + 8].astype(F32)
    return (td[0:1] + td[1:2] + td[2:3]) * td[3:4], td[4:5] + td[5:6] + td[6:7]


def pick(grad_part, value_part):
    lane = lax.broadcasted_iota(jnp.int32, grad_part.shape, 1)
    return jnp.where(lane < WIDTH, grad_part * SCALE, value_part * 0.25)


def widen(x):
    return jnp.concatenate([x, jnp.zeros((x.shape[0], 128 - x.shape[1]), F32)], axis=1)


def both(keep_ref, came_ref, j, low, high):
    return jnp.concatenate([keep_ref[j, low:high, :], came_ref[j, low:high, :]], axis=1)


def near_forward_kernel(off_ref, keep_ref, came_ref, near_ref, taken_ref, base_ref, acc_ref):
    first = OWN * lax.axis_index("core") + 4 * pl.program_id(0)

    blocks = []
    for j in range(4):
        kv_t = both(keep_ref, came_ref, j, 0, 2 * WIDTH)
        blocks.append((turn(kv_t), kv_t[WIDTH:], both(keep_ref, came_ref, j, 2 * WIDTH, 3 * WIDTH)))
    for j, (numerator, sums) in enumerate(forward_units(blocks)):
        block = sum_columns(numerator, sums, both(keep_ref, came_ref, j, 3 * WIDTH, TD))
        near_ref[j, :WIDTH, :] = numerator
        near_ref[j, WIDTH:, :] = block[DEN : DEN + 16]
        acc_ref[j * 512 : j * 512 + 512, :] = block.T

    row = lax.broadcasted_iota(jnp.int32, (TAKEN, 512), 0)
    col = lax.broadcasted_iota(jnp.int32, (TAKEN, 512), 1)
    is_two, is_three = row < 64, row < 72
    start = jnp.where(is_two, 8 * row, jnp.where(is_three, 64 * (row - 64), 256 * (row - 72)))
    for j in range(4):
        o2, o3, o4 = off_ref[0, first + j], off_ref[1, first + j], off_ref[2, first + j]
        base_ref[j, 64:, :] = jnp.ones((16, 128), F32)
        base_ref[j, :64, :] = acc_ref[pl.ds(j * 512 + o2, 64, stride=8), :]
        base_ref[j, 64:72, :] = acc_ref[pl.ds(j * 512 + o3, 8, stride=64), :]
        base_ref[j, 72:74, :] = acc_ref[pl.ds(j * 512 + o4, 2, stride=256), :]
        target = start + jnp.where(is_two, o2, jnp.where(is_three, o3, o4))
        hit = jnp.where(col == target, 1.0, 0.0).astype(BF16)
        picked = dot_t(hit, both(keep_ref, came_ref, j, 0, TD))
        picked = jnp.concatenate([picked, jnp.zeros((TAKEN, FAR_LANES - TD), F32)], axis=1)
        base = base_ref[j]
        total = base[:, DEN : DEN + 1]
        taken_ref[j] = with_sums(picked, total, base[:, LINED : LINED + 1] / total)


def middle_kernel(off_ref, in_ref, block2_ref, far_ref):
    head = OWN * lax.axis_index("core") + lax.axis_index(CHIPS)
    o2, o3, o4 = off_ref[0, head], off_ref[1, head], off_ref[2, head]
    two = jnp.concatenate([in_ref[s, :64, :] for s in range(OWN)], axis=0)
    two_t = turn(two)
    numerator, sums = forward_unit(two[:, : 2 * WIDTH], two_t[WIDTH : 2 * WIDTH], two_t[2 * WIDTH : 3 * WIDTH])
    block2_ref[...] = sum_rows(numerator, sums, two_t[3 * WIDTH : TD])

    rest = jnp.concatenate([in_ref[s, 64:, :] for s in range(OWN)], axis=0)
    row = lax.broadcasted_iota(jnp.int32, (PICK_FAR, 128), 0)
    col = lax.broadcasted_iota(jnp.int32, (PICK_FAR, 128), 1)
    four = row - PICK_THREE
    source = jnp.where(row < PICK_THREE, 16 * (row >> 3) + (row & 7), 16 * (four >> 1) + 8 + (four & 1))
    far = dot(jnp.where(col == source, 1.0, 0.0).astype(BF16), rest)
    total, dots = sums_beside(far)
    from2 = jnp.concatenate(
        [
            jnp.where((o3 & 7) == o2, block2_ref[pl.ds(o3 >> 3, PICK_THREE, stride=8), :], 0.0),
            jnp.where((o4 & 7) == o2, block2_ref[pl.ds(o4 >> 3, PICK_FOUR, stride=32), :], 0.0),
        ],
        axis=0,
    )
    lined = dots * total + from2[:, LINED : LINED + 1]
    total = total + from2[:, DEN : DEN + 1]
    low = fold(with_sums(far, total, lined / total))
    for s in range(8):
        far_ref[s] = low


def far_forward(far):
    far_t = turn(far)
    result = forward_unit(far[:, : 2 * WIDTH], far_t[WIDTH : 2 * WIDTH], far_t[2 * WIDTH : 3 * WIDTH])
    return far_t, sum_rows(*result, far_t[3 * WIDTH : TD])


def three_kernel(off_ref, all_ref, block3_ref, three_ref, four_ref):
    head = OWN * lax.axis_index("core") + lax.axis_index(CHIPS)
    o3, o4 = off_ref[1, head], off_ref[2, head]
    meet = (o4 & 63) == o3
    parts = [unfold(all_ref[j]) for j in range(8)]
    far3 = jnp.concatenate([part[0] for part in parts], axis=0)
    three_ref[...] = far3
    block3_ref[...] = far_forward(far3)[1]
    four = jnp.concatenate([part[1] for part in parts], axis=0).astype(F32)
    from3 = jnp.where(meet, block3_ref[pl.ds(o4 >> 6, 128, stride=4), :], 0.0)
    total, dots = sums_beside(four)
    lined = dots * total + from3[:, LINED : LINED + 1]
    total = total + from3[:, DEN : DEN + 1]
    four_ref[...] = with_sums(four, total, lined / total)


def totals_of(far_t, rows):
    near_total, near_dots = near_sums(far_t)
    far = rows.T
    total = near_total + far[DEN : DEN + 1]
    total = jnp.where(total > 0.0, total, 1.0)
    return 1.0 / (total * 0.25), (near_dots * near_total + far[LINED : LINED + 1]) / total


def far_kernel(
    off_ref, in_ref, block2_ref, far3_ref, block3_ref, here_ref, there_ref,
    out_ref, two_ref, three_ref, four_ref,
):
    head = OWN * lax.axis_index("core") + lax.axis_index(CHIPS)
    group = lax.axis_index(HALF)
    o2, o3, o4 = off_ref[0, head], off_ref[1, head], off_ref[2, head]
    meet = (o4 & 63) == o3
    own_rows3 = pl.ds(pl.multiple_of(group * PICK_THREE, PICK_THREE), PICK_THREE)
    own_rows4 = pl.ds(pl.multiple_of(group * PICK_FOUR, PICK_FOUR), PICK_FOUR)

    far3 = far3_ref[...]
    far3_t = turn(far3)
    far4 = jnp.concatenate([here_ref[...], there_ref[...]], axis=0)
    far4_t, block4 = far_forward(far4)
    four_ref[...] = block4
    three_ref[...] = block3_ref[...]
    same = pl.ds(o4 >> 6, 128, stride=4)
    three_ref[same, :] = three_ref[same, :] + jnp.where(meet, four_ref[:128, :], 0.0)

    own3 = three_ref[own_rows3, :]
    own4 = four_ref[own_rows4, :]
    only4 = jnp.where(meet, 0.0, own4)
    two_ref[...] = block2_ref[...]
    in_two = pl.ds(o3 >> 3, PICK_THREE, stride=8)
    two_ref[in_two, :] = two_ref[in_two, :] + jnp.where((o3 & 7) == o2, own3, 0.0)
    in_two = pl.ds(o4 >> 3, PICK_FOUR, stride=32)
    two_ref[in_two, :] = two_ref[in_two, :] + jnp.where((o4 & 7) == o2, only4, 0.0)

    two = jnp.concatenate([in_ref[s, :64, :] for s in range(OWN)], axis=0)
    two_t = turn(two)
    pad = 128 - PICK_FAR
    own = jnp.concatenate(
        [far3_ref[own_rows3, :], here_ref[own_rows4, :], jnp.zeros((pad, FAR_LANES), BF16)], axis=0
    )
    own_t = turn(own)
    own_block = jnp.concatenate([own3, own4, jnp.zeros((pad, 128), F32)], axis=0)
    inverse2, dots2 = totals_of(two_t, two_ref[...])
    inverse3, dots3 = totals_of(far3_t, three_ref[...])
    inverse4, dots4 = totals_of(far4_t, four_ref[...])
    own_inverse, own_dots = totals_of(own_t, own_block)

    def queries(turned):
        return turned[2 * WIDTH : 3 * WIDTH], turned[3 * WIDTH : TD]

    kv_own = own[:, : 2 * WIDTH]
    results = backward_units((
        (two[:, : 2 * WIDTH], *queries(two_t), inverse2, dots2),
        (far3[:, : 2 * WIDTH], *queries(own_t), own_inverse, own_dots),
        (far4[:, : 2 * WIDTH], *queries(own_t), own_inverse, own_dots),
        (kv_own, *queries(far3_t), inverse3, dots3),
        (kv_own, *queries(far4_t), inverse4, dots4),
    ))
    query2 = query_rows(dot(two_t[:WIDTH], results[0][1])) + block2_ref[...]
    query3 = query_rows(dot(far3_t[:WIDTH], results[1][1]))[:PICK_THREE] + own3
    query4 = query_rows(dot(far4_t[:WIDTH], results[2][1]))[PICK_THREE:PICK_FAR] + only4

    def keys(result, far):
        qg = far[:, 2 * WIDTH : TD]
        return widen(pick(dot(result[1], qg), dot(result[0], qg)))

    keys2 = keys(results[0], two)
    keys3 = keys(results[3], far3)[:PICK_THREE]
    keys4 = keys(results[4], far4)[PICK_THREE:PICK_FAR]
    for lanes, part2, part3, part4 in (
        (slice(0, 128), keys2, keys3, keys4),
        (slice(128, 256), query2, query3, query4),
    ):
        for c in range(OWN):
            out_ref[c, :64, lanes] = part2[64 * c : 64 * c + 64]
            out_ref[c, 64:72, lanes] = part3[8 * c : 8 * c + 8]
            out_ref[c, 72:74, lanes] = part4[2 * c : 2 * c + 2]
            out_ref[c, 74:, lanes] = jnp.zeros((TAKEN - 74, 128), F32)


def lone_backward_kernel(off_ref, keep_ref, came_ref, acc_ref, near_ref, keys_ref):
    first = OWN * lax.axis_index("core") + 2 * pl.program_id(0)
    blocks = []
    turned = []
    for j in range(2):
        kv_t = both(keep_ref, came_ref, j, 0, 2 * WIDTH)
        qg_t = both(keep_ref, came_ref, j, 2 * WIDTH, TD)
        sums = acc_ref[j]
        total = sums[WIDTH : WIDTH + 1]
        near_ref[j, :WIDTH, :] = (sums[:WIDTH] / total).astype(BF16)
        inverse = jnp.where(chosen_columns(off_ref, first + j), 0.0, 1.0 / (total * 0.25))
        blocks.append((turn(kv_t), qg_t[:WIDTH], qg_t[WIDTH:], inverse, sums[WIDTH + 8 : WIDTH + 9] / total))
        turned.append((kv_t[:WIDTH], turn(qg_t)))
    results = backward_units(blocks)
    query_parts = [dot(part[0], grad) * SCALE for part, (_, grad) in zip(turned, results)]
    grad_parts = [dot(grad, part[1]) for part, (_, grad) in zip(turned, results)]
    value_parts = [dot(share, part[1]) for part, (share, _) in zip(turned, results)]
    for j in range(2):
        near_ref[j, WIDTH:, :] = query_parts[j].astype(BF16)
        keys_ref[j * 512 : j * 512 + 512, :] = widen(pick(grad_parts[j], value_parts[j]))


def chosen_columns(off_ref, head):
    col = lax.broadcasted_iota(jnp.int32, (1, 512), 1)
    two = (col & 7) == off_ref[0, head]
    three = (col & 63) == off_ref[1, head]
    four = (col & 255) == off_ref[2, head]
    return jnp.logical_or(two, jnp.logical_or(three, four))


def last_backward_kernel(
    off_ref, keep_ref, came_ref, taken_ref, base_ref, back_ref, near_ref, lone_ref,
    stay_ref, leave_ref, rows_ref, keys_ref,
):
    first = OWN * lax.axis_index("core") + 4 * pl.program_id(0)
    rows_b = slice(128, 256)

    def put(j, low, high, value):
        stay_ref[j, low:high, :] = value[:, :ROWS]
        leave_ref[j, low:high, :] = value[:, ROWS:]

    def valid(place, three_in_two, four_in_more):
        is_three = jnp.logical_and(place >= 64, place < 72)
        is_four = jnp.logical_and(place >= 72, place < 74)
        lost = jnp.where(is_three, three_in_two, jnp.where(is_four, four_in_more, jnp.where(place < 64, 0, 1)))
        return lost == 0

    blocks = []
    rest = []
    for j in range(4):
        o2, o3, o4 = off_ref[0, first + j], off_ref[1, first + j], off_ref[2, first + j]
        three_in_two = (o3 & 7) == o2
        four_in_two = (o4 & 7) == o2
        meet = (o4 & 63) == o3
        only_three = jnp.logical_and(meet, jnp.logical_not(four_in_two))
        flags = (three_in_two.astype(jnp.int32), jnp.logical_or(meet, four_in_two).astype(jnp.int32))
        rows_ref[j, TAKEN:, :] = jnp.ones((128 - TAKEN, 128), F32)
        rows_ref[j, :TAKEN, :] = base_ref[j] + back_ref[j, :, rows_b]
        for rows, low, high, take in (
            (pl.ds(o3 >> 3, 8, stride=8), 64, 72, three_in_two),
            (pl.ds(o4 >> 3, 2, stride=32), 72, 74, four_in_two),
            (pl.ds(64 + (o4 >> 6), 2, stride=4), 72, 74, only_three),
        ):
            rows_ref[j, rows, :] = rows_ref[j, rows, :] + jnp.where(take, back_ref[j, low:high, rows_b], 0.0)
        sums = rows_ref[j].T
        total = sums[DEN : DEN + 1]
        lane = lax.broadcasted_iota(jnp.int32, (1, 128), 1)
        inverse = jnp.where(valid(lane, *flags), 1.0 / (total * 0.25), 0.0)
        taken = jnp.concatenate([taken_ref[j], jnp.zeros((128 - TAKEN, FAR_LANES), BF16)], axis=0)
        taken_t = turn(taken)
        kv_t = both(keep_ref, came_ref, j, 0, 2 * WIDTH)
        blocks.append((
            turn(kv_t), taken_t[2 * WIDTH : 3 * WIDTH], taken_t[3 * WIDTH : TD], inverse,
            sums[LINED : LINED + 1] / total,
        ))
        row = lax.broadcasted_iota(jnp.int32, (128, 512), 0)
        col = lax.broadcasted_iota(jnp.int32, (128, 512), 1)
        target = jnp.where(row < 64, 8 * row + o2, jnp.where(row < 72, 64 * (row - 64) + o3, 256 * (row - 72) + o4))
        hit = jnp.logical_and(col == target, valid(row, *flags))
        rest.append((
            kv_t[:WIDTH], taken[:, 2 * WIDTH : TD], sums[:WIDTH] / total, sums[WIDTH : 2 * WIDTH],
            jnp.where(hit, 1.0, 0.0).astype(BF16),
        ))
    results = backward_units(blocks)
    query_parts = [dot(part[0], grad) * SCALE + part[3] for part, (_, grad) in zip(rest, results)]
    grad_parts = [dot(grad, part[1]) for part, (_, grad) in zip(rest, results)]
    value_parts = [dot(share, part[1]) for part, (share, _) in zip(rest, results)]
    for j in range(4):
        low = jnp.concatenate([rest[j][2], query_parts[j]], axis=0).astype(BF16)
        spread = dot(low, rest[j][4])
        chosen = chosen_columns(off_ref, first + j)
        put(j, 0, 2 * WIDTH, jnp.where(chosen, spread, near_ref[j].astype(F32)).astype(BF16))
        base = j * 512
        keys_ref[base : base + 512, :] = lone_ref[base : base + 512, :] + widen(pick(grad_parts[j], value_parts[j]))
        for low, high, which, stride in ((0, 64, 0, 8), (64, 72, 1, 64), (72, 74, 2, 256)):
            rows = pl.ds(base + off_ref[which, first + j], high - low, stride=stride)
            keys_ref[rows, :] = keys_ref[rows, :] + back_ref[j, low:high, :128]
        put(j, 2 * WIDTH, TD, keys_ref[base : base + 512, :].astype(BF16).T[: 2 * WIDTH])


def per_device(queries, key_states, value_states, cotangent, offsets):
    struct = jax.ShapeDtypeStruct

    def in_hbm(x):
        return pltpu.with_memory_space_constraint(x, pltpu.HBM)

    queries, key_states, value_states, cotangent, offsets = map(
        in_hbm, (queries, key_states, value_states, cotangent, offsets)
    )
    def swap(x):
        return lax.ppermute(x, "core", [(0, 1), (1, 0)])

    half = struct((OWN, 4 * WIDTH, ROWS), BF16)
    arrays = (key_states, value_states, queries, cotangent)
    came = swap(pack_half(arrays, False, half))
    keep = pack_half(arrays, True, half)
    rows_f32 = pltpu.HBM((GROUP_ROWS, 128), F32)
    acc, picked, base = call(
        near_forward_kernel,
        (pltpu.HBM((OWN, 64, 512), F32), struct((OWN, TAKEN, FAR_LANES), BF16), pltpu.HBM((OWN, TAKEN, 128), F32)),
        scratch=(pltpu.VMEM((4 * 512, 128), F32),),
        steps=2,
        smem=1,
        args=(offsets, keep, came),
    )
    taken = lax.all_to_all(picked, CHIPS, 0, 0, tiled=True)
    block2, far = call(
        middle_kernel,
        (struct((PICK_TWO, 128), F32), struct((8, 128, 128), BF16)),
        smem=1,
        args=(offsets, taken),
    )
    far = lax.all_to_all(far, HALF, 0, 0, tiled=True)
    block3, far3, here = call(
        three_kernel,
        (struct((512, 128), F32), struct((512, FAR_LANES), BF16), struct((128, FAR_LANES), BF16)),
        smem=1,
        args=(offsets, far),
    )
    there = lax.ppermute(here, "y_high", [(0, 1), (1, 0)])
    back = call(
        far_kernel,
        struct((OWN, TAKEN, 256), F32),
        scratch=(pltpu.VMEM((512, 128), F32), pltpu.VMEM((512, 128), F32), pltpu.VMEM((256, 128), F32)),
        smem=1,
        args=(offsets, taken, block2, far3, block3, here, there),
    )
    back = lax.all_to_all(back, CHIPS, 0, 0, tiled=True)
    near, lone = call(
        lone_backward_kernel,
        (struct((OWN, 2 * WIDTH, 512), BF16), rows_f32),
        steps=4,
        smem=1,
        args=(offsets, keep, came, in_hbm(acc)),
    )
    stay, leave = call(
        last_backward_kernel,
        (half, half),
        scratch=(pltpu.VMEM((4, 128, 128), F32), pltpu.VMEM((2048, 128), F32)),
        steps=2,
        smem=1,
        args=(offsets, keep, came, picked, in_hbm(base), back, near, in_hbm(lone)),
    )
    came = swap(leave)
    outs = unpack_half(stay, True, ())
    return tuple(unpack_half(came, False, tuple(map(in_hbm, outs))))


def solution(mesh):
    axes = ("y_high", "y_low", "z_high", "z_low", "x", "core")
    inner = Mesh(mesh.devices.reshape(2, 2, 4, 2, 4, 2), axes)
    rows = P(axes, None)
    return jax.shard_map(
        per_device,
        mesh=inner,
        in_specs=(rows, rows, rows, rows, P()),
        out_specs=(rows, rows, rows, rows),
        check_vma=False,
    )
```

```python
import functools
import math

import jax
import jax.numpy as jnp
from jax import lax
from jax.experimental import pallas as pl
from jax.experimental.pallas import tpu as pltpu
from jax.sharding import Mesh, PartitionSpec as P

HEADS = 16
WIDTH = 48
ROWS = 256
HALF_WIDTH = 384
OWN = 8
GROUP_ROWS = 16 * ROWS
PICK_TWO = GROUP_ROWS // 8
PICK_THREE = GROUP_ROWS // 64
PICK_FOUR = GROUP_ROWS // 256
PICK_FAR = PICK_THREE + PICK_FOUR
FACTOR = WIDTH**-0.5
EXPONENT = FACTOR * math.log2(math.e)
BF16 = jnp.bfloat16
F32 = jnp.float32
LIMIT = 32 * 1024 * 1024

CHIPS = ("z_low", "x")
HALF = ("y_low", "z_high")


def dot(a, b):
    return lax.dot_general(a, b, (((1,), (0,)), ((), ())), preferred_element_type=F32)


def dot_t(a, b):
    return lax.dot_general(a, b, (((1,), (1,)), ((), ())), preferred_element_type=F32)


def call(kernel, out_shape, scratch=(), smem=0, args=(), steps=0):
    smem_spec = pl.BlockSpec(memory_space=pltpu.SMEM)

    def spec(array):
        if not steps:
            return pl.BlockSpec(memory_space=pltpu.VMEM)
        rest = array.shape[1:]
        return pl.BlockSpec((array.shape[0] // steps, *rest), lambda i: (i,) + (0,) * len(rest))

    return pl.pallas_call(
        kernel,
        out_shape=out_shape,
        grid=(steps,) if steps else (),
        in_specs=[smem_spec] * smem + [spec(array) for array in args[smem:]],
        out_specs=jax.tree.map(spec, out_shape),
        scratch_shapes=list(scratch),
        compiler_params=pltpu.CompilerParams(vmem_limit_bytes=LIMIT),
    )(*args)


def half_columns(core):
    return pl.ds(pl.multiple_of(core * HALF_WIDTH, HALF_WIDTH), HALF_WIDTH)


def pack_half(arrays, own, half):
    def kernel(k_ref, v_ref, q_ref, g_ref, out_ref, raw_ref, sem_ref):
        core = lax.axis_index("core")
        columns = half_columns(core if own else 1 - core)
        copies = [
            pltpu.make_async_copy(ref.at[:, columns], raw_ref.at[place], sem_ref.at[place])
            for place, ref in enumerate((k_ref, v_ref, q_ref, g_ref))
        ]
        for copy in copies:
            copy.start()
        for place, copy in enumerate(copies):
            copy.wait()
            out_ref[:, place * WIDTH : (place + 1) * WIDTH, :] = raw_ref[place].T.reshape(OWN, WIDTH, ROWS)

    return pl.pallas_call(
        kernel,
        out_shape=half,
        in_specs=[pl.BlockSpec(memory_space=pl.ANY)] * 4,
        out_specs=pl.BlockSpec(memory_space=pltpu.VMEM),
        scratch_shapes=[pltpu.VMEM((4, ROWS, HALF_WIDTH), BF16), pltpu.SemaphoreType.DMA((4,))],
        compiler_params=pltpu.CompilerParams(vmem_limit_bytes=LIMIT),
    )(*arrays)


def unpack_half(half, own, outs):
    shape = pltpu.HBM((ROWS, HEADS * WIDTH), BF16)

    def kernel(in_ref, *refs):
        out_refs, raw_ref, sem_ref = refs[-6:-2], refs[-2], refs[-1]
        core = lax.axis_index("core")
        columns = half_columns(core if own else 1 - core)
        copies = []
        for place, ref in enumerate(out_refs):
            block = in_ref[:, place * WIDTH : (place + 1) * WIDTH, :].reshape(HALF_WIDTH, ROWS)
            raw_ref[place] = block.T
            copy = pltpu.make_async_copy(raw_ref.at[place], ref.at[:, columns], sem_ref.at[place])
            copy.start()
            copies.append(copy)
        for copy in copies:
            copy.wait()

    anywhere = pl.BlockSpec(memory_space=pl.ANY)
    return pl.pallas_call(
        kernel,
        out_shape=(shape,) * 4,
        in_specs=[pl.BlockSpec(memory_space=pltpu.VMEM)] + [anywhere] * len(outs),
        out_specs=(anywhere,) * 4,
        input_output_aliases={place + 1: place for place in range(len(outs))},
        scratch_shapes=[pltpu.VMEM((4, ROWS, HALF_WIDTH), BF16), pltpu.SemaphoreType.DMA((4,))],
        compiler_params=pltpu.CompilerParams(vmem_limit_bytes=LIMIT),
    )(half, *outs)


def upper(q_t):
    return jnp.concatenate([q_t, jnp.zeros_like(q_t)], axis=0)


def lower(g_t):
    return jnp.concatenate([jnp.zeros_like(g_t), g_t], axis=0)


def forward_units(blocks):
    scores = [dot(kv, upper(q_t)) for kv, _, q_t in blocks]
    weights = [jnp.exp2(score * EXPONENT) for score in scores]
    sums = [jnp.sum(weight, axis=0, keepdims=True) for weight in weights]
    low = [(weight * (1.0 / (total * 0.25))).astype(BF16) for weight, total in zip(weights, sums)]
    outputs = [dot(block[1], probs) * 0.25 for block, probs in zip(blocks, low)]
    return [(output * total, total) for output, total in zip(outputs, sums)]


def forward_unit(kv, v_t, q_t):
    middle = q_t.shape[1] // 2
    parts = forward_units([(kv, v_t, q_t[:, :middle]), (kv, v_t, q_t[:, middle:])])
    return tuple(jnp.concatenate(pieces, axis=1) for pieces in zip(*parts))


def backward_units(blocks):
    scores = [dot(block[0], upper(block[1])) for block in blocks]
    probs = [dot(block[0], lower(block[2])) for block in blocks]
    shares = [jnp.exp2(score * EXPONENT) * block[3] for score, block in zip(scores, blocks)]
    grads = [(share * (prob - block[4])).astype(BF16) for share, prob, block in zip(shares, probs, blocks)]
    return [(share.astype(BF16), grad) for share, grad in zip(shares, grads)]


def backward_unit(kv, q_t, g_t, inverse, dots):
    return backward_units([(kv, q_t, g_t, inverse, dots)])[0]


def turn(x):
    return x.T


FAR_LANES = 256
TD = 4 * WIDTH
DEN = 96
LINED = 104
TAKEN = 80
SCALE = FACTOR * 0.25


def thirds(x):
    high = x.astype(BF16).astype(F32)
    rest = x - high
    middle = rest.astype(BF16).astype(F32)
    return high, middle, rest - middle


def sum_columns(numerator, sums, g_t):
    count = numerator.shape[1]
    lined = jnp.sum(g_t.astype(F32) * numerator, axis=0, keepdims=True)
    return jnp.concatenate(
        [
            numerator,
            jnp.zeros((WIDTH, count), F32),
            jnp.broadcast_to(sums, (8, count)),
            jnp.broadcast_to(lined, (24, count)),
        ],
        axis=0,
    )


def sum_rows(numerator, sums, g_t):
    return sum_columns(numerator, sums, g_t).T


def query_rows(part_t):
    count = part_t.shape[1]
    return jnp.concatenate([jnp.zeros((WIDTH, count), F32), part_t * SCALE, jnp.zeros((32, count), F32)], axis=0).T


def with_sums(picked, total, dots):
    large, small = total > 2.0**60, total < 2.0**-60
    level = jnp.where(large, 2.0**64, jnp.where(small, 2.0**-64, 1.0))
    unlevel = jnp.where(large, 2.0**-64, jnp.where(small, 2.0**64, 1.0))
    lane = lax.broadcasted_iota(jnp.int32, picked.shape, 1)
    for place, column in enumerate((*thirds(total * unlevel), level, *thirds(dots))):
        picked = jnp.where(lane == TD + place, column, picked)
    return picked.astype(BF16)


def fold(rows):
    tail = rows[:, 128:]
    pairs = jnp.concatenate([tail[:32, :64], tail[32:64, :64]], axis=1)
    sums = [tail[16 * i : 16 * i + 16, 64:72] for i in range(4)]
    last = jnp.concatenate([tail[64:, :72], *sums, jnp.zeros((16, 24), rows.dtype)], axis=1)
    return jnp.concatenate([rows[:, :128], pairs, last], axis=0)


def unfold(block):
    pairs, last = block[80:112], block[112:]
    tail = jnp.concatenate([pairs[:, :64], pairs[:, 64:]], axis=0)
    sums = jnp.concatenate([last[:, 72 + 8 * i : 80 + 8 * i] for i in range(4)], axis=0)
    three = jnp.concatenate([block[:64], tail, sums, jnp.zeros((64, 56), block.dtype)], axis=1)
    four = jnp.concatenate([block[64:80], last[:, :72], jnp.zeros((16, 56), block.dtype)], axis=1)
    return three, four


def sums_beside(far):
    def column(place):
        return far[:, TD + place : TD + place + 1]

    return (column(0) + column(1) + column(2)) * column(3), column(4) + column(5) + column(6)


def near_sums(far_t):
    td = far_t[TD : TD + 8].astype(F32)
    return (td[0:1] + td[1:2] + td[2:3]) * td[3:4], td[4:5] + td[5:6] + td[6:7]


def pick(grad_part, value_part):
    lane = lax.broadcasted_iota(jnp.int32, grad_part.shape, 1)
    return jnp.where(lane < WIDTH, grad_part * SCALE, value_part * 0.25)


def widen(x):
    return jnp.concatenate([x, jnp.zeros((x.shape[0], 128 - x.shape[1]), F32)], axis=1)


def both(keep_ref, came_ref, j, low, high):
    return jnp.concatenate([keep_ref[j, low:high, :], came_ref[j, low:high, :]], axis=1)


def taken_kernel(off_ref, keep_ref, came_ref, taken_ref, base_ref):
    first = OWN * lax.axis_index("core")
    row = lax.broadcasted_iota(jnp.int32, (TAKEN, 512), 0)
    col = lax.broadcasted_iota(jnp.int32, (TAKEN, 512), 1)
    is_two, is_three = row < 64, row < 72
    start = jnp.where(is_two, 8 * row, jnp.where(is_three, 64 * (row - 64), 256 * (row - 72)))
    blocks = []
    rows = []
    for j in range(8):
        o2, o3, o4 = off_ref[0, first + j], off_ref[1, first + j], off_ref[2, first + j]
        target = start + jnp.where(is_two, o2, jnp.where(is_three, o3, o4))
        hit = jnp.where(col == target, 1.0, 0.0).astype(BF16)
        columns = both(keep_ref, came_ref, j, 0, TD)
        picked = dot_t(hit, columns)
        picked_t = turn(jnp.concatenate([picked.astype(BF16), jnp.zeros((128 - TAKEN, TD), BF16)], axis=0))
        kv_t = columns[: 2 * WIDTH]
        blocks.append((turn(kv_t), kv_t[WIDTH:], picked_t[2 * WIDTH : 3 * WIDTH]))
        rows.append((picked, picked_t[3 * WIDTH :]))
    for j, (numerator, sums) in enumerate(forward_units(blocks)):
        picked, g_t = rows[j]
        base = sum_rows(numerator, sums, g_t)[:TAKEN]
        base_ref[j] = base
        picked = jnp.concatenate([picked, jnp.zeros((TAKEN, FAR_LANES - TD), F32)], axis=1)
        total = base[:, DEN : DEN + 1]
        taken_ref[j] = with_sums(picked, total, base[:, LINED : LINED + 1] / total)


def middle_kernel(off_ref, in_ref, block2_ref, far_ref):
    head = OWN * lax.axis_index("core") + lax.axis_index(CHIPS)
    o2, o3, o4 = off_ref[0, head], off_ref[1, head], off_ref[2, head]
    two = jnp.concatenate([in_ref[s, :64, :] for s in range(OWN)], axis=0)
    two_t = turn(two)
    numerator, sums = forward_unit(two[:, : 2 * WIDTH], two_t[WIDTH : 2 * WIDTH], two_t[2 * WIDTH : 3 * WIDTH])
    block2_ref[...] = sum_rows(numerator, sums, two_t[3 * WIDTH : TD])

    rest = jnp.concatenate([in_ref[s, 64:, :] for s in range(OWN)], axis=0)
    row = lax.broadcasted_iota(jnp.int32, (PICK_FAR, 128), 0)
    col = lax.broadcasted_iota(jnp.int32, (PICK_FAR, 128), 1)
    four = row - PICK_THREE
    source = jnp.where(row < PICK_THREE, 16 * (row >> 3) + (row & 7), 16 * (four >> 1) + 8 + (four & 1))
    far = dot(jnp.where(col == source, 1.0, 0.0).astype(BF16), rest)
    total, dots = sums_beside(far)
    from2 = jnp.concatenate(
        [
            jnp.where((o3 & 7) == o2, block2_ref[pl.ds(o3 >> 3, PICK_THREE, stride=8), :], 0.0),
            jnp.where((o4 & 7) == o2, block2_ref[pl.ds(o4 >> 3, PICK_FOUR, stride=32), :], 0.0),
        ],
        axis=0,
    )
    lined = dots * total + from2[:, LINED : LINED + 1]
    total = total + from2[:, DEN : DEN + 1]
    low = fold(with_sums(far, total, lined / total))
    for s in range(8):
        far_ref[s] = low


def far_forward(far):
    far_t = turn(far)
    result = forward_unit(far[:, : 2 * WIDTH], far_t[WIDTH : 2 * WIDTH], far_t[2 * WIDTH : 3 * WIDTH])
    return far_t, sum_rows(*result, far_t[3 * WIDTH : TD])


def three_kernel(off_ref, all_ref, block3_ref, three_ref, four_ref):
    head = OWN * lax.axis_index("core") + lax.axis_index(CHIPS)
    o3, o4 = off_ref[1, head], off_ref[2, head]
    meet = (o4 & 63) == o3
    parts = [unfold(all_ref[j]) for j in range(8)]
    far3 = jnp.concatenate([part[0] for part in parts], axis=0)
    three_ref[...] = far3
    block3_ref[...] = far_forward(far3)[1]
    four = jnp.concatenate([part[1] for part in parts], axis=0).astype(F32)
    from3 = jnp.where(meet, block3_ref[pl.ds(o4 >> 6, 128, stride=4), :], 0.0)
    total, dots = sums_beside(four)
    lined = dots * total + from3[:, LINED : LINED + 1]
    total = total + from3[:, DEN : DEN + 1]
    four_ref[...] = with_sums(four, total, lined / total)


def totals_of(far_t, rows):
    near_total, near_dots = near_sums(far_t)
    far = rows.T
    total = near_total + far[DEN : DEN + 1]
    total = jnp.where(total > 0.0, total, 1.0)
    return 1.0 / (total * 0.25), (near_dots * near_total + far[LINED : LINED + 1]) / total


def far_kernel(
    off_ref, in_ref, block2_ref, far3_ref, block3_ref, here_ref, there_ref,
    out_ref, two_ref, three_ref, four_ref,
):
    head = OWN * lax.axis_index("core") + lax.axis_index(CHIPS)
    group = lax.axis_index(HALF)
    o2, o3, o4 = off_ref[0, head], off_ref[1, head], off_ref[2, head]
    meet = (o4 & 63) == o3
    own_rows3 = pl.ds(pl.multiple_of(group * PICK_THREE, PICK_THREE), PICK_THREE)
    own_rows4 = pl.ds(pl.multiple_of(group * PICK_FOUR, PICK_FOUR), PICK_FOUR)

    far3 = far3_ref[...]
    far3_t = turn(far3)
    far4 = jnp.concatenate([here_ref[...], there_ref[...]], axis=0)
    far4_t, block4 = far_forward(far4)
    four_ref[...] = block4
    three_ref[...] = block3_ref[...]
    same = pl.ds(o4 >> 6, 128, stride=4)
    three_ref[same, :] = three_ref[same, :] + jnp.where(meet, four_ref[:128, :], 0.0)

    own3 = three_ref[own_rows3, :]
    own4 = four_ref[own_rows4, :]
    only4 = jnp.where(meet, 0.0, own4)
    two_ref[...] = block2_ref[...]
    in_two = pl.ds(o3 >> 3, PICK_THREE, stride=8)
    two_ref[in_two, :] = two_ref[in_two, :] + jnp.where((o3 & 7) == o2, own3, 0.0)
    in_two = pl.ds(o4 >> 3, PICK_FOUR, stride=32)
    two_ref[in_two, :] = two_ref[in_two, :] + jnp.where((o4 & 7) == o2, only4, 0.0)

    two = jnp.concatenate([in_ref[s, :64, :] for s in range(OWN)], axis=0)
    two_t = turn(two)
    pad = 128 - PICK_FAR
    own = jnp.concatenate(
        [far3_ref[own_rows3, :], here_ref[own_rows4, :], jnp.zeros((pad, FAR_LANES), BF16)], axis=0
    )
    own_t = turn(own)
    own_block = jnp.concatenate([own3, own4, jnp.zeros((pad, 128), F32)], axis=0)
    inverse2, dots2 = totals_of(two_t, two_ref[...])
    inverse3, dots3 = totals_of(far3_t, three_ref[...])
    inverse4, dots4 = totals_of(far4_t, four_ref[...])
    own_inverse, own_dots = totals_of(own_t, own_block)

    def queries(turned):
        return turned[2 * WIDTH : 3 * WIDTH], turned[3 * WIDTH : TD]

    kv_own = own[:, : 2 * WIDTH]
    results = backward_units((
        (two[:, : 2 * WIDTH], *queries(two_t), inverse2, dots2),
        (far3[:, : 2 * WIDTH], *queries(own_t), own_inverse, own_dots),
        (far4[:, : 2 * WIDTH], *queries(own_t), own_inverse, own_dots),
        (kv_own, *queries(far3_t), inverse3, dots3),
        (kv_own, *queries(far4_t), inverse4, dots4),
    ))
    query2 = query_rows(dot(two_t[:WIDTH], results[0][1])) + block2_ref[...]
    query3 = query_rows(dot(far3_t[:WIDTH], results[1][1]))[:PICK_THREE] + own3
    query4 = query_rows(dot(far4_t[:WIDTH], results[2][1]))[PICK_THREE:PICK_FAR] + only4

    def keys(result, far):
        qg = far[:, 2 * WIDTH : TD]
        return widen(pick(dot(result[1], qg), dot(result[0], qg)))

    keys2 = keys(results[0], two)
    keys3 = keys(results[3], far3)[:PICK_THREE]
    keys4 = keys(results[4], far4)[PICK_THREE:PICK_FAR]
    for lanes, part2, part3, part4 in (
        (slice(0, 128), keys2, keys3, keys4),
        (slice(128, 256), query2, query3, query4),
    ):
        for c in range(OWN):
            out_ref[c, :64, lanes] = part2[64 * c : 64 * c + 64]
            out_ref[c, 64:72, lanes] = part3[8 * c : 8 * c + 8]
            out_ref[c, 72:74, lanes] = part4[2 * c : 2 * c + 2]
            out_ref[c, 74:, lanes] = jnp.zeros((TAKEN - 74, 128), F32)


def lone_kernel(first_step, off_ref, keep_ref, came_ref, *refs):
    near_ref, keys_ref = refs[-2:]
    first = OWN * lax.axis_index("core") + 2 * (first_step + pl.program_id(0))
    blocks = []
    for j in range(2):
        kv_t = both(keep_ref, came_ref, j, 0, 2 * WIDTH)
        qg_t = both(keep_ref, came_ref, j, 2 * WIDTH, TD)
        blocks.append((turn(kv_t), kv_t, qg_t, turn(qg_t)))
    scores = [dot(kv, upper(qg_t[:WIDTH])) for kv, _, qg_t, _ in blocks]
    probs = [dot(kv, lower(qg_t[WIDTH:])) for kv, _, qg_t, _ in blocks]
    weights = [jnp.exp2(score * EXPONENT) for score in scores]
    shares = []
    for j, weight in enumerate(weights):
        inverse = 1.0 / (jnp.sum(weight, axis=0, keepdims=True) * 0.25)
        shares.append(weight * jnp.where(chosen_columns(off_ref, first + j), 0.0, inverse))
    low = [share.astype(BF16) for share in shares]
    merged = [dot(block[1][WIDTH:], share) * 0.25 for block, share in zip(blocks, low)]
    dots = [
        jnp.sum(block[2][WIDTH:].astype(F32) * part, axis=0, keepdims=True) for block, part in zip(blocks, merged)
    ]
    grads = [(share * (prob - line)).astype(BF16) for share, prob, line in zip(shares, probs, dots)]
    query_parts = [dot(block[1][:WIDTH], grad) * SCALE for block, grad in zip(blocks, grads)]
    grad_parts = [dot(grad, block[3]) for block, grad in zip(blocks, grads)]
    value_parts = [dot(share, block[3]) for block, share in zip(blocks, low)]
    for j in range(2):
        near_ref[j, :WIDTH, :] = merged[j].astype(BF16)
        near_ref[j, WIDTH:, :] = query_parts[j].astype(BF16)
        keys_ref[j * 512 : j * 512 + 512, :] = widen(pick(grad_parts[j], value_parts[j]))


def lone_half(first_step, offsets, keep, came, filled):
    def spec(*shape):
        return pl.BlockSpec(shape, lambda i: (first_step + i,) + (0,) * (len(shape) - 1))

    heads = spec(2, 4 * WIDTH, ROWS)
    return pl.pallas_call(
        functools.partial(lone_kernel, first_step),
        out_shape=(pltpu.HBM((OWN, 2 * WIDTH, 512), BF16), pltpu.HBM((GROUP_ROWS, 128), F32)),
        grid=(2,),
        in_specs=[pl.BlockSpec(memory_space=pltpu.SMEM), heads, heads]
        + [pl.BlockSpec(memory_space=pl.ANY)] * len(filled),
        out_specs=(spec(2, 2 * WIDTH, 512), spec(1024, 128)),
        input_output_aliases={3 + place: place for place in range(len(filled))},
        compiler_params=pltpu.CompilerParams(vmem_limit_bytes=LIMIT),
    )(offsets, keep, came, *filled)


def chosen_columns(off_ref, head):
    col = lax.broadcasted_iota(jnp.int32, (1, 512), 1)
    two = (col & 7) == off_ref[0, head]
    three = (col & 63) == off_ref[1, head]
    four = (col & 255) == off_ref[2, head]
    return jnp.logical_or(two, jnp.logical_or(three, four))


def last_backward_kernel(
    off_ref, keep_ref, came_ref, taken_ref, base_ref, back_ref, near_ref, lone_ref,
    stay_ref, leave_ref, rows_ref, keys_ref,
):
    first = OWN * lax.axis_index("core") + 4 * pl.program_id(0)
    rows_b = slice(128, 256)

    def put(j, low, high, value):
        stay_ref[j, low:high, :] = value[:, :ROWS]
        leave_ref[j, low:high, :] = value[:, ROWS:]

    def valid(place, three_in_two, four_in_more):
        is_three = jnp.logical_and(place >= 64, place < 72)
        is_four = jnp.logical_and(place >= 72, place < 74)
        lost = jnp.where(is_three, three_in_two, jnp.where(is_four, four_in_more, jnp.where(place < 64, 0, 1)))
        return lost == 0

    blocks = []
    rest = []
    for j in range(4):
        o2, o3, o4 = off_ref[0, first + j], off_ref[1, first + j], off_ref[2, first + j]
        three_in_two = (o3 & 7) == o2
        four_in_two = (o4 & 7) == o2
        meet = (o4 & 63) == o3
        only_three = jnp.logical_and(meet, jnp.logical_not(four_in_two))
        flags = (three_in_two.astype(jnp.int32), jnp.logical_or(meet, four_in_two).astype(jnp.int32))
        rows_ref[j, TAKEN:, :] = jnp.ones((128 - TAKEN, 128), F32)
        rows_ref[j, :TAKEN, :] = base_ref[j] + back_ref[j, :, rows_b]
        for rows, low, high, take in (
            (pl.ds(o3 >> 3, 8, stride=8), 64, 72, three_in_two),
            (pl.ds(o4 >> 3, 2, stride=32), 72, 74, four_in_two),
            (pl.ds(64 + (o4 >> 6), 2, stride=4), 72, 74, only_three),
        ):
            rows_ref[j, rows, :] = rows_ref[j, rows, :] + jnp.where(take, back_ref[j, low:high, rows_b], 0.0)
        sums = rows_ref[j].T
        total = sums[DEN : DEN + 1]
        lane = lax.broadcasted_iota(jnp.int32, (1, 128), 1)
        inverse = jnp.where(valid(lane, *flags), 1.0 / (total * 0.25), 0.0)
        taken = jnp.concatenate([taken_ref[j], jnp.zeros((128 - TAKEN, FAR_LANES), BF16)], axis=0)
        taken_t = turn(taken)
        kv_t = both(keep_ref, came_ref, j, 0, 2 * WIDTH)
        blocks.append((
            turn(kv_t), taken_t[2 * WIDTH : 3 * WIDTH], taken_t[3 * WIDTH : TD], inverse,
            sums[LINED : LINED + 1] / total,
        ))
        row = lax.broadcasted_iota(jnp.int32, (128, 512), 0)
        col = lax.broadcasted_iota(jnp.int32, (128, 512), 1)
        target = jnp.where(row < 64, 8 * row + o2, jnp.where(row < 72, 64 * (row - 64) + o3, 256 * (row - 72) + o4))
        hit = jnp.logical_and(col == target, valid(row, *flags))
        rest.append((
            kv_t[:WIDTH], taken[:, 2 * WIDTH : TD], sums[:WIDTH] / total, sums[WIDTH : 2 * WIDTH],
            jnp.where(hit, 1.0, 0.0).astype(BF16),
        ))
    results = backward_units(blocks)
    query_parts = [dot(part[0], grad) * SCALE + part[3] for part, (_, grad) in zip(rest, results)]
    grad_parts = [dot(grad, part[1]) for part, (_, grad) in zip(rest, results)]
    value_parts = [dot(share, part[1]) for part, (share, _) in zip(rest, results)]
    for j in range(4):
        low = jnp.concatenate([rest[j][2], query_parts[j]], axis=0).astype(BF16)
        spread = dot(low, rest[j][4])
        chosen = chosen_columns(off_ref, first + j)
        put(j, 0, 2 * WIDTH, jnp.where(chosen, spread, near_ref[j].astype(F32)).astype(BF16))
        base = j * 512
        keys_ref[base : base + 512, :] = lone_ref[base : base + 512, :] + widen(pick(grad_parts[j], value_parts[j]))
        for low, high, which, stride in ((0, 64, 0, 8), (64, 72, 1, 64), (72, 74, 2, 256)):
            rows = pl.ds(base + off_ref[which, first + j], high - low, stride=stride)
            keys_ref[rows, :] = keys_ref[rows, :] + back_ref[j, low:high, :128]
        put(j, 2 * WIDTH, TD, keys_ref[base : base + 512, :].astype(BF16).T[: 2 * WIDTH])


def per_device(queries, key_states, value_states, cotangent, offsets):
    struct = jax.ShapeDtypeStruct

    def in_hbm(x):
        return pltpu.with_memory_space_constraint(x, pltpu.HBM)

    def in_vmem(x):
        return pltpu.with_memory_space_constraint(x, pltpu.VMEM)

    queries, key_states, value_states, cotangent, offsets = map(
        in_hbm, (queries, key_states, value_states, cotangent, offsets)
    )
    def swap(x):
        return lax.ppermute(x, "core", [(0, 1), (1, 0)])

    half = struct((OWN, 4 * WIDTH, ROWS), BF16)
    arrays = (key_states, value_states, queries, cotangent)
    came = swap(pack_half(arrays, False, half))
    keep = pack_half(arrays, True, half)
    rows_f32 = pltpu.HBM((GROUP_ROWS, 128), F32)
    picked, base = call(
        taken_kernel,
        (struct((OWN, TAKEN, FAR_LANES), BF16), pltpu.HBM((OWN, TAKEN, 128), F32)),
        steps=0,
        smem=1,
        args=(offsets, keep, came),
    )
    taken = in_vmem(lax.all_to_all(picked, CHIPS, 0, 0, tiled=True))
    near, lone = lone_half(0, offsets, keep, came, ())
    taken, near, lone = lax.optimization_barrier((taken, near, lone))
    block2, far = call(
        middle_kernel,
        (struct((PICK_TWO, 128), F32), struct((8, 128, 128), BF16)),
        smem=1,
        args=(offsets, taken),
    )
    far = lax.all_to_all(far, HALF, 0, 0, tiled=True)
    block3, far3, here = call(
        three_kernel,
        (struct((512, 128), F32), struct((512, FAR_LANES), BF16), struct((128, FAR_LANES), BF16)),
        smem=1,
        args=(offsets, far),
    )
    there = lax.ppermute(here, "y_high", [(0, 1), (1, 0)])
    back = call(
        far_kernel,
        struct((OWN, TAKEN, 256), F32),
        scratch=(pltpu.VMEM((512, 128), F32), pltpu.VMEM((512, 128), F32), pltpu.VMEM((256, 128), F32)),
        smem=1,
        args=(offsets, taken, block2, far3, block3, here, there),
    )
    back = in_vmem(lax.all_to_all(back, CHIPS, 0, 0, tiled=True))
    near, lone = lone_half(2, offsets, keep, came, (in_hbm(near), in_hbm(lone)))
    stay, leave = call(
        last_backward_kernel,
        (half, half),
        scratch=(pltpu.VMEM((4, 128, 128), F32), pltpu.VMEM((2048, 128), F32)),
        steps=2,
        smem=1,
        args=(offsets, keep, came, picked, in_hbm(base), back, in_hbm(near), in_hbm(lone)),
    )
    came = swap(leave)
    outs = unpack_half(stay, True, ())
    return tuple(unpack_half(came, False, tuple(map(in_hbm, outs))))


def solution(mesh):
    axes = ("y_high", "y_low", "z_high", "z_low", "x", "core")
    inner = Mesh(mesh.devices.reshape(2, 2, 4, 2, 4, 2), axes)
    rows = P(axes, None)
    return jax.shard_map(
        per_device,
        mesh=inner,
        in_specs=(rows, rows, rows, rows, P()),
        out_specs=(rows, rows, rows, rows),
        check_vma=False,
    )
```

```python
import functools
import math

import jax
import jax.numpy as jnp
from jax import lax
from jax.experimental import pallas as pl
from jax.experimental.pallas import tpu as pltpu
from jax.sharding import Mesh, PartitionSpec as P

HEADS = 16
WIDTH = 48
ROWS = 256
HALF_WIDTH = 384
OWN = 8
GROUP_ROWS = 16 * ROWS
PICK_TWO = GROUP_ROWS // 8
PICK_THREE = GROUP_ROWS // 64
PICK_FOUR = GROUP_ROWS // 256
PICK_FAR = PICK_THREE + PICK_FOUR
FACTOR = WIDTH**-0.5
EXPONENT = FACTOR * math.log2(math.e)
BF16 = jnp.bfloat16
F32 = jnp.float32
LIMIT = 32 * 1024 * 1024

CHIPS = ("z_low", "x")
HALF = ("y_low", "z_high")


def dot(a, b):
    return lax.dot_general(a, b, (((1,), (0,)), ((), ())), preferred_element_type=F32)


def dot_t(a, b):
    return lax.dot_general(a, b, (((1,), (1,)), ((), ())), preferred_element_type=F32)


def call(kernel, out_shape, scratch=(), smem=0, args=(), steps=0):
    smem_spec = pl.BlockSpec(memory_space=pltpu.SMEM)

    def spec(array):
        if not steps:
            return pl.BlockSpec(memory_space=pltpu.VMEM)
        rest = array.shape[1:]
        return pl.BlockSpec((array.shape[0] // steps, *rest), lambda i: (i,) + (0,) * len(rest))

    return pl.pallas_call(
        kernel,
        out_shape=out_shape,
        grid=(steps,) if steps else (),
        in_specs=[smem_spec] * smem + [spec(array) for array in args[smem:]],
        out_specs=jax.tree.map(spec, out_shape),
        scratch_shapes=list(scratch),
        compiler_params=pltpu.CompilerParams(vmem_limit_bytes=LIMIT),
    )(*args)


def half_columns(core):
    return pl.ds(pl.multiple_of(core * HALF_WIDTH, HALF_WIDTH), HALF_WIDTH)


def pack_half(arrays, own, half):
    def kernel(k_ref, v_ref, q_ref, g_ref, out_ref, raw_ref, sem_ref):
        core = lax.axis_index("core")
        columns = half_columns(core if own else 1 - core)
        copies = [
            pltpu.make_async_copy(ref.at[:, columns], raw_ref.at[place], sem_ref.at[place])
            for place, ref in enumerate((k_ref, v_ref, q_ref, g_ref))
        ]
        for copy in copies:
            copy.start()
        for place, copy in enumerate(copies):
            copy.wait()
            out_ref[:, place * WIDTH : (place + 1) * WIDTH, :] = raw_ref[place].T.reshape(OWN, WIDTH, ROWS)

    return pl.pallas_call(
        kernel,
        out_shape=half,
        in_specs=[pl.BlockSpec(memory_space=pl.ANY)] * 4,
        out_specs=pl.BlockSpec(memory_space=pltpu.VMEM),
        scratch_shapes=[pltpu.VMEM((4, ROWS, HALF_WIDTH), BF16), pltpu.SemaphoreType.DMA((4,))],
        compiler_params=pltpu.CompilerParams(vmem_limit_bytes=LIMIT),
    )(*arrays)


def unpack_half(half, own, outs):
    shape = pltpu.HBM((ROWS, HEADS * WIDTH), BF16)

    def kernel(in_ref, *refs):
        out_refs, raw_ref, sem_ref = refs[-6:-2], refs[-2], refs[-1]
        core = lax.axis_index("core")
        columns = half_columns(core if own else 1 - core)
        copies = []
        for place, ref in enumerate(out_refs):
            block = in_ref[:, place * WIDTH : (place + 1) * WIDTH, :].reshape(HALF_WIDTH, ROWS)
            raw_ref[place] = block.T
            copy = pltpu.make_async_copy(raw_ref.at[place], ref.at[:, columns], sem_ref.at[place])
            copy.start()
            copies.append(copy)
        for copy in copies:
            copy.wait()

    anywhere = pl.BlockSpec(memory_space=pl.ANY)
    return pl.pallas_call(
        kernel,
        out_shape=(shape,) * 4,
        in_specs=[pl.BlockSpec(memory_space=pltpu.VMEM)] + [anywhere] * len(outs),
        out_specs=(anywhere,) * 4,
        input_output_aliases={place + 1: place for place in range(len(outs))},
        scratch_shapes=[pltpu.VMEM((4, ROWS, HALF_WIDTH), BF16), pltpu.SemaphoreType.DMA((4,))],
        compiler_params=pltpu.CompilerParams(vmem_limit_bytes=LIMIT),
    )(half, *outs)


def upper(q_t):
    return jnp.concatenate([q_t, jnp.zeros_like(q_t)], axis=0)


def lower(g_t):
    return jnp.concatenate([jnp.zeros_like(g_t), g_t], axis=0)


def forward_units(blocks):
    scores = [dot(kv, upper(q_t)) for kv, _, q_t in blocks]
    weights = [jnp.exp2(score * EXPONENT) for score in scores]
    sums = [jnp.sum(weight, axis=0, keepdims=True) for weight in weights]
    low = [(weight * (1.0 / (total * 0.25))).astype(BF16) for weight, total in zip(weights, sums)]
    outputs = [dot(block[1], probs) * 0.25 for block, probs in zip(blocks, low)]
    return [(output * total, total) for output, total in zip(outputs, sums)]


def forward_unit(kv, v_t, q_t):
    middle = q_t.shape[1] // 2
    parts = forward_units([(kv, v_t, q_t[:, :middle]), (kv, v_t, q_t[:, middle:])])
    return tuple(jnp.concatenate(pieces, axis=1) for pieces in zip(*parts))


def backward_units(blocks):
    scores = [dot(block[0], upper(block[1])) for block in blocks]
    probs = [dot(block[0], lower(block[2])) for block in blocks]
    shares = [jnp.exp2(score * EXPONENT) * block[3] for score, block in zip(scores, blocks)]
    grads = [(share * (prob - block[4])).astype(BF16) for share, prob, block in zip(shares, probs, blocks)]
    return [(share.astype(BF16), grad) for share, grad in zip(shares, grads)]


def backward_unit(kv, q_t, g_t, inverse, dots):
    return backward_units([(kv, q_t, g_t, inverse, dots)])[0]


def turn(x):
    return x.T


FAR_LANES = 256
TD = 4 * WIDTH
DEN = 96
LINED = 104
TAKEN = 80
SCALE = FACTOR * 0.25


def thirds(x):
    high = x.astype(BF16).astype(F32)
    rest = x - high
    middle = rest.astype(BF16).astype(F32)
    return high, middle, rest - middle


def sum_columns(numerator, sums, g_t):
    count = numerator.shape[1]
    lined = jnp.sum(g_t.astype(F32) * numerator, axis=0, keepdims=True)
    return jnp.concatenate(
        [
            numerator,
            jnp.zeros((WIDTH, count), F32),
            jnp.broadcast_to(sums, (8, count)),
            jnp.broadcast_to(lined, (24, count)),
        ],
        axis=0,
    )


def sum_rows(numerator, sums, g_t):
    return sum_columns(numerator, sums, g_t).T


def query_rows(part_t):
    count = part_t.shape[1]
    return jnp.concatenate([jnp.zeros((WIDTH, count), F32), part_t * SCALE, jnp.zeros((32, count), F32)], axis=0).T


def with_sums(picked, total, dots):
    large, small = total > 2.0**60, total < 2.0**-60
    level = jnp.where(large, 2.0**64, jnp.where(small, 2.0**-64, 1.0))
    unlevel = jnp.where(large, 2.0**-64, jnp.where(small, 2.0**64, 1.0))
    lane = lax.broadcasted_iota(jnp.int32, picked.shape, 1)
    for place, column in enumerate((*thirds(total * unlevel), level, *thirds(dots))):
        picked = jnp.where(lane == TD + place, column, picked)
    return picked.astype(BF16)


def fold(rows):
    tail = rows[:, 128:]
    pairs = jnp.concatenate([tail[:32, :64], tail[32:64, :64]], axis=1)
    sums = [tail[16 * i : 16 * i + 16, 64:72] for i in range(4)]
    last = jnp.concatenate([tail[64:, :72], *sums, jnp.zeros((16, 24), rows.dtype)], axis=1)
    return jnp.concatenate([rows[:, :128], pairs, last], axis=0)


def unfold(block):
    pairs, last = block[80:112], block[112:]
    tail = jnp.concatenate([pairs[:, :64], pairs[:, 64:]], axis=0)
    sums = jnp.concatenate([last[:, 72 + 8 * i : 80 + 8 * i] for i in range(4)], axis=0)
    three = jnp.concatenate([block[:64], tail, sums, jnp.zeros((64, 56), block.dtype)], axis=1)
    four = jnp.concatenate([block[64:80], last[:, :72], jnp.zeros((16, 56), block.dtype)], axis=1)
    return three, four


def sums_beside(far):
    def column(place):
        return far[:, TD + place : TD + place + 1]

    return (column(0) + column(1) + column(2)) * column(3), column(4) + column(5) + column(6)


def near_sums(far_t):
    td = far_t[TD : TD + 8].astype(F32)
    return (td[0:1] + td[1:2] + td[2:3]) * td[3:4], td[4:5] + td[5:6] + td[6:7]


def pick(grad_part, value_part):
    lane = lax.broadcasted_iota(jnp.int32, grad_part.shape, 1)
    return jnp.where(lane < WIDTH, grad_part * SCALE, value_part * 0.25)


def widen(x):
    return jnp.concatenate([x, jnp.zeros((x.shape[0], 128 - x.shape[1]), F32)], axis=1)


def both(keep_ref, came_ref, j, low, high):
    return jnp.concatenate([keep_ref[j, low:high, :], came_ref[j, low:high, :]], axis=1)


def taken_kernel(off_ref, keep_ref, came_ref, taken_ref, base_ref):
    first = OWN * lax.axis_index("core")
    row = lax.broadcasted_iota(jnp.int32, (TAKEN, 512), 0)
    col = lax.broadcasted_iota(jnp.int32, (TAKEN, 512), 1)
    is_two, is_three = row < 64, row < 72
    start = jnp.where(is_two, 8 * row, jnp.where(is_three, 64 * (row - 64), 256 * (row - 72)))
    blocks = []
    rows = []
    for j in range(8):
        o2, o3, o4 = off_ref[0, first + j], off_ref[1, first + j], off_ref[2, first + j]
        target = start + jnp.where(is_two, o2, jnp.where(is_three, o3, o4))
        hit = jnp.where(col == target, 1.0, 0.0).astype(BF16)
        columns = both(keep_ref, came_ref, j, 0, TD)
        picked = dot_t(hit, columns)
        picked_t = turn(jnp.concatenate([picked.astype(BF16), jnp.zeros((128 - TAKEN, TD), BF16)], axis=0))
        kv_t = columns[: 2 * WIDTH]
        blocks.append((turn(kv_t), kv_t[WIDTH:], picked_t[2 * WIDTH : 3 * WIDTH]))
        rows.append((picked, picked_t[3 * WIDTH :]))
    for j, (numerator, sums) in enumerate(forward_units(blocks)):
        picked, g_t = rows[j]
        base = sum_rows(numerator, sums, g_t)[:TAKEN]
        base_ref[j] = base
        picked = jnp.concatenate([picked, jnp.zeros((TAKEN, FAR_LANES - TD), F32)], axis=1)
        total = base[:, DEN : DEN + 1]
        taken_ref[j] = with_sums(picked, total, base[:, LINED : LINED + 1] / total)


def middle_kernel(off_ref, in_ref, block2_ref, far_ref):
    head = OWN * lax.axis_index("core") + lax.axis_index(CHIPS)
    o2, o3, o4 = off_ref[0, head], off_ref[1, head], off_ref[2, head]
    two = jnp.concatenate([in_ref[s, :64, :] for s in range(OWN)], axis=0)
    two_t = turn(two)
    numerator, sums = forward_unit(two[:, : 2 * WIDTH], two_t[WIDTH : 2 * WIDTH], two_t[2 * WIDTH : 3 * WIDTH])
    block2_ref[...] = sum_rows(numerator, sums, two_t[3 * WIDTH : TD])

    rest = jnp.concatenate([in_ref[s, 64:, :] for s in range(OWN)], axis=0)
    row = lax.broadcasted_iota(jnp.int32, (PICK_FAR, 128), 0)
    col = lax.broadcasted_iota(jnp.int32, (PICK_FAR, 128), 1)
    four = row - PICK_THREE
    source = jnp.where(row < PICK_THREE, 16 * (row >> 3) + (row & 7), 16 * (four >> 1) + 8 + (four & 1))
    far = dot(jnp.where(col == source, 1.0, 0.0).astype(BF16), rest)
    total, dots = sums_beside(far)
    from2 = jnp.concatenate(
        [
            jnp.where((o3 & 7) == o2, block2_ref[pl.ds(o3 >> 3, PICK_THREE, stride=8), :], 0.0),
            jnp.where((o4 & 7) == o2, block2_ref[pl.ds(o4 >> 3, PICK_FOUR, stride=32), :], 0.0),
        ],
        axis=0,
    )
    lined = dots * total + from2[:, LINED : LINED + 1]
    total = total + from2[:, DEN : DEN + 1]
    low = fold(with_sums(far, total, lined / total))
    for s in range(8):
        far_ref[s] = low


def far_forward(far):
    far_t = turn(far)
    result = forward_unit(far[:, : 2 * WIDTH], far_t[WIDTH : 2 * WIDTH], far_t[2 * WIDTH : 3 * WIDTH])
    return far_t, sum_rows(*result, far_t[3 * WIDTH : TD])


def three_kernel(off_ref, all_ref, block3_ref, three_ref, four_ref):
    head = OWN * lax.axis_index("core") + lax.axis_index(CHIPS)
    o3, o4 = off_ref[1, head], off_ref[2, head]
    meet = (o4 & 63) == o3
    parts = [unfold(all_ref[j]) for j in range(8)]
    far3 = jnp.concatenate([part[0] for part in parts], axis=0)
    three_ref[...] = far3
    block3_ref[...] = far_forward(far3)[1]
    four = jnp.concatenate([part[1] for part in parts], axis=0).astype(F32)
    from3 = jnp.where(meet, block3_ref[pl.ds(o4 >> 6, 128, stride=4), :], 0.0)
    total, dots = sums_beside(four)
    lined = dots * total + from3[:, LINED : LINED + 1]
    total = total + from3[:, DEN : DEN + 1]
    four_ref[...] = with_sums(four, total, lined / total)


def totals_of(far_t, rows):
    near_total, near_dots = near_sums(far_t)
    far = rows.T
    total = near_total + far[DEN : DEN + 1]
    total = jnp.where(total > 0.0, total, 1.0)
    return 1.0 / (total * 0.25), (near_dots * near_total + far[LINED : LINED + 1]) / total


def ahead_kernel(in_ref, far3_ref, two_ref, two_t_ref, far3_t_ref, weights_ref, probs_ref):
    two = jnp.concatenate([in_ref[s, :64, :] for s in range(OWN)], axis=0)
    two_t = turn(two)
    two_ref[...] = two
    two_t_ref[...] = two_t
    far3_t_ref[...] = turn(far3_ref[...])
    kv = two[:, : 2 * WIDTH]
    weights_ref[...] = jnp.exp2(dot(kv, upper(two_t[2 * WIDTH : 3 * WIDTH])) * EXPONENT)
    probs_ref[...] = dot(kv, lower(two_t[3 * WIDTH : TD]))


def far_kernel(
    off_ref, two_in_ref, two_t_ref, far3_t_ref, weights_ref, probs_ref,
    block2_ref, far3_ref, block3_ref, here_ref, there_ref,
    out_ref, two_ref, three_ref, four_ref,
):
    head = OWN * lax.axis_index("core") + lax.axis_index(CHIPS)
    group = lax.axis_index(HALF)
    o2, o3, o4 = off_ref[0, head], off_ref[1, head], off_ref[2, head]
    meet = (o4 & 63) == o3
    own_rows3 = pl.ds(pl.multiple_of(group * PICK_THREE, PICK_THREE), PICK_THREE)
    own_rows4 = pl.ds(pl.multiple_of(group * PICK_FOUR, PICK_FOUR), PICK_FOUR)

    far3 = far3_ref[...]
    far3_t = far3_t_ref[...]
    far4 = jnp.concatenate([here_ref[...], there_ref[...]], axis=0)
    far4_t, block4 = far_forward(far4)
    four_ref[...] = block4
    three_ref[...] = block3_ref[...]
    same = pl.ds(o4 >> 6, 128, stride=4)
    three_ref[same, :] = three_ref[same, :] + jnp.where(meet, four_ref[:128, :], 0.0)

    own3 = three_ref[own_rows3, :]
    own4 = four_ref[own_rows4, :]
    only4 = jnp.where(meet, 0.0, own4)
    two_ref[...] = block2_ref[...]
    in_two = pl.ds(o3 >> 3, PICK_THREE, stride=8)
    two_ref[in_two, :] = two_ref[in_two, :] + jnp.where((o3 & 7) == o2, own3, 0.0)
    in_two = pl.ds(o4 >> 3, PICK_FOUR, stride=32)
    two_ref[in_two, :] = two_ref[in_two, :] + jnp.where((o4 & 7) == o2, only4, 0.0)

    two = two_in_ref[...]
    two_t = two_t_ref[...]
    pad = 128 - PICK_FAR
    own = jnp.concatenate(
        [far3_ref[own_rows3, :], here_ref[own_rows4, :], jnp.zeros((pad, FAR_LANES), BF16)], axis=0
    )
    own_t = turn(own)
    own_block = jnp.concatenate([own3, own4, jnp.zeros((pad, 128), F32)], axis=0)
    inverse2, dots2 = totals_of(two_t, two_ref[...])
    inverse3, dots3 = totals_of(far3_t, three_ref[...])
    inverse4, dots4 = totals_of(far4_t, four_ref[...])
    own_inverse, own_dots = totals_of(own_t, own_block)

    def queries(turned):
        return turned[2 * WIDTH : 3 * WIDTH], turned[3 * WIDTH : TD]

    kv_own = own[:, : 2 * WIDTH]
    shares2 = weights_ref[...] * inverse2
    result2 = (shares2.astype(BF16), (shares2 * (probs_ref[...] - dots2)).astype(BF16))
    results = [result2] + backward_units((
        (far3[:, : 2 * WIDTH], *queries(own_t), own_inverse, own_dots),
        (far4[:, : 2 * WIDTH], *queries(own_t), own_inverse, own_dots),
        (kv_own, *queries(far3_t), inverse3, dots3),
        (kv_own, *queries(far4_t), inverse4, dots4),
    ))
    query2 = query_rows(dot(two_t[:WIDTH], results[0][1])) + block2_ref[...]
    query3 = query_rows(dot(far3_t[:WIDTH], results[1][1]))[:PICK_THREE] + own3
    query4 = query_rows(dot(far4_t[:WIDTH], results[2][1]))[PICK_THREE:PICK_FAR] + only4

    def keys(result, far):
        qg = far[:, 2 * WIDTH : TD]
        return widen(pick(dot(result[1], qg), dot(result[0], qg)))

    keys2 = keys(results[0], two)
    keys3 = keys(results[3], far3)[:PICK_THREE]
    keys4 = keys(results[4], far4)[PICK_THREE:PICK_FAR]
    for lanes, part2, part3, part4 in (
        (slice(0, 128), keys2, keys3, keys4),
        (slice(128, 256), query2, query3, query4),
    ):
        for c in range(OWN):
            out_ref[c, :64, lanes] = part2[64 * c : 64 * c + 64]
            out_ref[c, 64:72, lanes] = part3[8 * c : 8 * c + 8]
            out_ref[c, 72:74, lanes] = part4[2 * c : 2 * c + 2]
            out_ref[c, 74:, lanes] = jnp.zeros((TAKEN - 74, 128), F32)


def lone_kernel(first_step, off_ref, keep_ref, came_ref, *refs):
    near_ref, keys_ref = refs[-2:]
    first = OWN * lax.axis_index("core") + 2 * (first_step + pl.program_id(0))
    blocks = []
    for j in range(2):
        kv_t = both(keep_ref, came_ref, j, 0, 2 * WIDTH)
        qg_t = both(keep_ref, came_ref, j, 2 * WIDTH, TD)
        blocks.append((turn(kv_t), kv_t, qg_t, turn(qg_t)))
    scores = [dot(kv, upper(qg_t[:WIDTH])) for kv, _, qg_t, _ in blocks]
    probs = [dot(kv, lower(qg_t[WIDTH:])) for kv, _, qg_t, _ in blocks]
    weights = [jnp.exp2(score * EXPONENT) for score in scores]
    shares = []
    for j, weight in enumerate(weights):
        inverse = 1.0 / (jnp.sum(weight, axis=0, keepdims=True) * 0.25)
        shares.append(weight * jnp.where(chosen_columns(off_ref, first + j), 0.0, inverse))
    low = [share.astype(BF16) for share in shares]
    merged = [dot(block[1][WIDTH:], share) * 0.25 for block, share in zip(blocks, low)]
    dots = [
        jnp.sum(block[2][WIDTH:].astype(F32) * part, axis=0, keepdims=True) for block, part in zip(blocks, merged)
    ]
    grads = [(share * (prob - line)).astype(BF16) for share, prob, line in zip(shares, probs, dots)]
    query_parts = [dot(block[1][:WIDTH], grad) * SCALE for block, grad in zip(blocks, grads)]
    grad_parts = [dot(grad, block[3]) for block, grad in zip(blocks, grads)]
    value_parts = [dot(share, block[3]) for block, share in zip(blocks, low)]
    for j in range(2):
        near_ref[j, :WIDTH, :] = merged[j].astype(BF16)
        near_ref[j, WIDTH:, :] = query_parts[j].astype(BF16)
        keys_ref[j * 512 : j * 512 + 512, :] = widen(pick(grad_parts[j], value_parts[j]))


def lone_half(first_step, offsets, keep, came, filled):
    def spec(*shape):
        return pl.BlockSpec(shape, lambda i: (first_step + i,) + (0,) * (len(shape) - 1))

    heads = spec(2, 4 * WIDTH, ROWS)
    return pl.pallas_call(
        functools.partial(lone_kernel, first_step),
        out_shape=(pltpu.HBM((OWN, 2 * WIDTH, 512), BF16), pltpu.HBM((GROUP_ROWS, 128), F32)),
        grid=(2,),
        in_specs=[pl.BlockSpec(memory_space=pltpu.SMEM), heads, heads]
        + [pl.BlockSpec(memory_space=pl.ANY)] * len(filled),
        out_specs=(spec(2, 2 * WIDTH, 512), spec(1024, 128)),
        input_output_aliases={3 + place: place for place in range(len(filled))},
        compiler_params=pltpu.CompilerParams(vmem_limit_bytes=LIMIT),
    )(offsets, keep, came, *filled)


def chosen_columns(off_ref, head):
    col = lax.broadcasted_iota(jnp.int32, (1, 512), 1)
    two = (col & 7) == off_ref[0, head]
    three = (col & 63) == off_ref[1, head]
    four = (col & 255) == off_ref[2, head]
    return jnp.logical_or(two, jnp.logical_or(three, four))


def last_backward_kernel(
    off_ref, keep_ref, came_ref, taken_ref, base_ref, back_ref, near_ref, lone_ref,
    stay_ref, leave_ref, rows_ref, keys_ref,
):
    first = OWN * lax.axis_index("core") + 4 * pl.program_id(0)
    rows_b = slice(128, 256)

    def put(j, low, high, value):
        stay_ref[j, low:high, :] = value[:, :ROWS]
        leave_ref[j, low:high, :] = value[:, ROWS:]

    def valid(place, three_in_two, four_in_more):
        is_three = jnp.logical_and(place >= 64, place < 72)
        is_four = jnp.logical_and(place >= 72, place < 74)
        lost = jnp.where(is_three, three_in_two, jnp.where(is_four, four_in_more, jnp.where(place < 64, 0, 1)))
        return lost == 0

    blocks = []
    rest = []
    for j in range(4):
        o2, o3, o4 = off_ref[0, first + j], off_ref[1, first + j], off_ref[2, first + j]
        three_in_two = (o3 & 7) == o2
        four_in_two = (o4 & 7) == o2
        meet = (o4 & 63) == o3
        only_three = jnp.logical_and(meet, jnp.logical_not(four_in_two))
        flags = (three_in_two.astype(jnp.int32), jnp.logical_or(meet, four_in_two).astype(jnp.int32))
        rows_ref[j, TAKEN:, :] = jnp.ones((128 - TAKEN, 128), F32)
        rows_ref[j, :TAKEN, :] = base_ref[j] + back_ref[j, :, rows_b]
        for rows, low, high, take in (
            (pl.ds(o3 >> 3, 8, stride=8), 64, 72, three_in_two),
            (pl.ds(o4 >> 3, 2, stride=32), 72, 74, four_in_two),
            (pl.ds(64 + (o4 >> 6), 2, stride=4), 72, 74, only_three),
        ):
            rows_ref[j, rows, :] = rows_ref[j, rows, :] + jnp.where(take, back_ref[j, low:high, rows_b], 0.0)
        sums = rows_ref[j].T
        total = sums[DEN : DEN + 1]
        lane = lax.broadcasted_iota(jnp.int32, (1, 128), 1)
        inverse = jnp.where(valid(lane, *flags), 1.0 / (total * 0.25), 0.0)
        taken = jnp.concatenate([taken_ref[j], jnp.zeros((128 - TAKEN, FAR_LANES), BF16)], axis=0)
        taken_t = turn(taken)
        kv_t = both(keep_ref, came_ref, j, 0, 2 * WIDTH)
        blocks.append((
            turn(kv_t), taken_t[2 * WIDTH : 3 * WIDTH], taken_t[3 * WIDTH : TD], inverse,
            sums[LINED : LINED + 1] / total,
        ))
        row = lax.broadcasted_iota(jnp.int32, (128, 512), 0)
        col = lax.broadcasted_iota(jnp.int32, (128, 512), 1)
        target = jnp.where(row < 64, 8 * row + o2, jnp.where(row < 72, 64 * (row - 64) + o3, 256 * (row - 72) + o4))
        hit = jnp.logical_and(col == target, valid(row, *flags))
        rest.append((
            kv_t[:WIDTH], taken[:, 2 * WIDTH : TD], sums[:WIDTH] / total, sums[WIDTH : 2 * WIDTH],
            jnp.where(hit, 1.0, 0.0).astype(BF16),
        ))
    results = backward_units(blocks)
    query_parts = [dot(part[0], grad) * SCALE + part[3] for part, (_, grad) in zip(rest, results)]
    grad_parts = [dot(grad, part[1]) for part, (_, grad) in zip(rest, results)]
    value_parts = [dot(share, part[1]) for part, (share, _) in zip(rest, results)]
    for j in range(4):
        low = jnp.concatenate([rest[j][2], query_parts[j]], axis=0).astype(BF16)
        spread = dot(low, rest[j][4])
        chosen = chosen_columns(off_ref, first + j)
        put(j, 0, 2 * WIDTH, jnp.where(chosen, spread, near_ref[j].astype(F32)).astype(BF16))
        base = j * 512
        keys_ref[base : base + 512, :] = lone_ref[base : base + 512, :] + widen(pick(grad_parts[j], value_parts[j]))
        for low, high, which, stride in ((0, 64, 0, 8), (64, 72, 1, 64), (72, 74, 2, 256)):
            rows = pl.ds(base + off_ref[which, first + j], high - low, stride=stride)
            keys_ref[rows, :] = keys_ref[rows, :] + back_ref[j, low:high, :128]
        put(j, 2 * WIDTH, TD, keys_ref[base : base + 512, :].astype(BF16).T[: 2 * WIDTH])


def per_device(queries, key_states, value_states, cotangent, offsets):
    struct = jax.ShapeDtypeStruct

    def in_hbm(x):
        return pltpu.with_memory_space_constraint(x, pltpu.HBM)

    def in_vmem(x):
        return pltpu.with_memory_space_constraint(x, pltpu.VMEM)

    queries, key_states, value_states, cotangent, offsets = map(
        in_hbm, (queries, key_states, value_states, cotangent, offsets)
    )
    def swap(x):
        return lax.ppermute(x, "core", [(0, 1), (1, 0)])

    half = struct((OWN, 4 * WIDTH, ROWS), BF16)
    arrays = (key_states, value_states, queries, cotangent)
    came = swap(pack_half(arrays, False, half))
    keep = pack_half(arrays, True, half)
    rows_f32 = pltpu.HBM((GROUP_ROWS, 128), F32)
    picked, base = call(
        taken_kernel,
        (struct((OWN, TAKEN, FAR_LANES), BF16), pltpu.HBM((OWN, TAKEN, 128), F32)),
        steps=0,
        smem=1,
        args=(offsets, keep, came),
    )
    taken = in_vmem(lax.all_to_all(picked, CHIPS, 0, 0, tiled=True))
    near, lone = lone_half(0, offsets, keep, came, ())
    taken, near, lone = lax.optimization_barrier((taken, near, lone))
    block2, far = call(
        middle_kernel,
        (struct((PICK_TWO, 128), F32), struct((8, 128, 128), BF16)),
        smem=1,
        args=(offsets, taken),
    )
    far = lax.all_to_all(far, HALF, 0, 0, tiled=True)
    block3, far3, here = call(
        three_kernel,
        (struct((512, 128), F32), struct((512, FAR_LANES), BF16), struct((128, FAR_LANES), BF16)),
        smem=1,
        args=(offsets, far),
    )
    there = lax.ppermute(here, "y_high", [(0, 1), (1, 0)])
    square = struct((512, 512), F32)
    turned = struct((FAR_LANES, 512), BF16)
    ahead = call(
        ahead_kernel,
        (struct((512, FAR_LANES), BF16), turned, turned, square, square),
        args=(taken, far3),
    )
    back = call(
        far_kernel,
        struct((OWN, TAKEN, 256), F32),
        scratch=(pltpu.VMEM((512, 128), F32), pltpu.VMEM((512, 128), F32), pltpu.VMEM((256, 128), F32)),
        smem=1,
        args=(offsets, *ahead, block2, far3, block3, here, there),
    )
    back = in_vmem(lax.all_to_all(back, CHIPS, 0, 0, tiled=True))
    near, lone = lone_half(2, offsets, keep, came, (in_hbm(near), in_hbm(lone)))
    stay, leave = call(
        last_backward_kernel,
        (half, half),
        scratch=(pltpu.VMEM((4, 128, 128), F32), pltpu.VMEM((2048, 128), F32)),
        steps=2,
        smem=1,
        args=(offsets, keep, came, picked, in_hbm(base), back, in_hbm(near), in_hbm(lone)),
    )
    came = swap(leave)
    outs = unpack_half(stay, True, ())
    return tuple(unpack_half(came, False, tuple(map(in_hbm, outs))))


def solution(mesh):
    axes = ("y_high", "y_low", "z_high", "z_low", "x", "core")
    inner = Mesh(mesh.devices.reshape(2, 2, 4, 2, 4, 2), axes)
    rows = P(axes, None)
    return jax.shard_map(
        per_device,
        mesh=inner,
        in_specs=(rows, rows, rows, rows, P()),
        out_specs=(rows, rows, rows, rows),
        check_vma=False,
    )
```

```python
import functools
import math

import jax
import jax.numpy as jnp
from jax import lax
from jax.experimental import pallas as pl
from jax.experimental.pallas import tpu as pltpu
from jax.sharding import Mesh, PartitionSpec as P

HEADS = 16
WIDTH = 48
ROWS = 256
HALF_WIDTH = 384
OWN = 8
GROUP_ROWS = 16 * ROWS
PICK_TWO = GROUP_ROWS // 8
PICK_THREE = GROUP_ROWS // 64
PICK_FOUR = GROUP_ROWS // 256
PICK_FAR = PICK_THREE + PICK_FOUR
FACTOR = WIDTH**-0.5
EXPONENT = FACTOR * math.log2(math.e)
BF16 = jnp.bfloat16
F32 = jnp.float32
LIMIT = 24 * 1024 * 1024

CHIPS = ("z_low", "x")
HALF = ("y_low", "z_high")


def dot(a, b):
    return lax.dot_general(a, b, (((1,), (0,)), ((), ())), preferred_element_type=F32)


def dot_t(a, b):
    return lax.dot_general(a, b, (((1,), (1,)), ((), ())), preferred_element_type=F32)


def call(kernel, out_shape, scratch=(), smem=0, args=(), steps=0):
    smem_spec = pl.BlockSpec(memory_space=pltpu.SMEM)

    def spec(array):
        if not steps:
            return pl.BlockSpec(memory_space=pltpu.VMEM)
        rest = array.shape[1:]
        return pl.BlockSpec((array.shape[0] // steps, *rest), lambda i: (i,) + (0,) * len(rest))

    return pl.pallas_call(
        kernel,
        out_shape=out_shape,
        grid=(steps,) if steps else (),
        in_specs=[smem_spec] * smem + [spec(array) for array in args[smem:]],
        out_specs=jax.tree.map(spec, out_shape),
        scratch_shapes=list(scratch),
        compiler_params=pltpu.CompilerParams(vmem_limit_bytes=LIMIT),
    )(*args)


def half_columns(core):
    return pl.ds(pl.multiple_of(core * HALF_WIDTH, HALF_WIDTH), HALF_WIDTH)


def pack_half(arrays, own, half):
    def kernel(k_ref, v_ref, q_ref, g_ref, out_ref, raw_ref, sem_ref):
        core = lax.axis_index("core")
        columns = half_columns(core if own else 1 - core)
        copies = [
            pltpu.make_async_copy(ref.at[:, columns], raw_ref.at[place], sem_ref.at[place])
            for place, ref in enumerate((k_ref, v_ref, q_ref, g_ref))
        ]
        for copy in copies:
            copy.start()
        for place, copy in enumerate(copies):
            copy.wait()
            out_ref[:, place * WIDTH : (place + 1) * WIDTH, :] = raw_ref[place].T.reshape(OWN, WIDTH, ROWS)

    return pl.pallas_call(
        kernel,
        out_shape=half,
        in_specs=[pl.BlockSpec(memory_space=pl.ANY)] * 4,
        out_specs=pl.BlockSpec(memory_space=pltpu.VMEM),
        scratch_shapes=[pltpu.VMEM((4, ROWS, HALF_WIDTH), BF16), pltpu.SemaphoreType.DMA((4,))],
        compiler_params=pltpu.CompilerParams(vmem_limit_bytes=LIMIT),
    )(*arrays)


def unpack_half(half, own, outs):
    shape = pltpu.HBM((ROWS, HEADS * WIDTH), BF16)

    def kernel(in_ref, *refs):
        out_refs, raw_ref, sem_ref = refs[-6:-2], refs[-2], refs[-1]
        core = lax.axis_index("core")
        columns = half_columns(core if own else 1 - core)
        copies = []
        for place, ref in enumerate(out_refs):
            block = in_ref[:, place * WIDTH : (place + 1) * WIDTH, :].reshape(HALF_WIDTH, ROWS)
            raw_ref[place] = block.T
            copy = pltpu.make_async_copy(raw_ref.at[place], ref.at[:, columns], sem_ref.at[place])
            copy.start()
            copies.append(copy)
        for copy in copies:
            copy.wait()

    anywhere = pl.BlockSpec(memory_space=pl.ANY)
    return pl.pallas_call(
        kernel,
        out_shape=(shape,) * 4,
        in_specs=[pl.BlockSpec(memory_space=pltpu.VMEM)] + [anywhere] * len(outs),
        out_specs=(anywhere,) * 4,
        input_output_aliases={place + 1: place for place in range(len(outs))},
        scratch_shapes=[pltpu.VMEM((4, ROWS, HALF_WIDTH), BF16), pltpu.SemaphoreType.DMA((4,))],
        compiler_params=pltpu.CompilerParams(vmem_limit_bytes=LIMIT),
    )(half, *outs)


def upper(q_t):
    return jnp.concatenate([q_t, jnp.zeros_like(q_t)], axis=0)


def lower(g_t):
    return jnp.concatenate([jnp.zeros_like(g_t), g_t], axis=0)


def forward_units(blocks):
    scores = [dot(kv, upper(q_t)) for kv, _, q_t in blocks]
    weights = [jnp.exp2(score * EXPONENT) for score in scores]
    sums = [jnp.sum(weight, axis=0, keepdims=True) for weight in weights]
    low = [(weight * (1.0 / (total * 0.25))).astype(BF16) for weight, total in zip(weights, sums)]
    outputs = [dot(block[1], probs) * 0.25 for block, probs in zip(blocks, low)]
    return [(output * total, total) for output, total in zip(outputs, sums)]


def forward_unit(kv, v_t, q_t):
    middle = q_t.shape[1] // 2
    parts = forward_units([(kv, v_t, q_t[:, :middle]), (kv, v_t, q_t[:, middle:])])
    return tuple(jnp.concatenate(pieces, axis=1) for pieces in zip(*parts))


def backward_units(blocks):
    scores = [dot(block[0], upper(block[1])) for block in blocks]
    probs = [dot(block[0], lower(block[2])) for block in blocks]
    shares = [jnp.exp2(score * EXPONENT) * block[3] for score, block in zip(scores, blocks)]
    grads = [(share * (prob - block[4])).astype(BF16) for share, prob, block in zip(shares, probs, blocks)]
    return [(share.astype(BF16), grad) for share, grad in zip(shares, grads)]


def backward_unit(kv, q_t, g_t, inverse, dots):
    return backward_units([(kv, q_t, g_t, inverse, dots)])[0]


def turn(x):
    return x.T


FAR_LANES = 256
TD = 4 * WIDTH
DEN = 96
LINED = 104
TAKEN = 80
SCALE = FACTOR * 0.25


def thirds(x):
    high = x.astype(BF16).astype(F32)
    rest = x - high
    middle = rest.astype(BF16).astype(F32)
    return high, middle, rest - middle


def sum_columns(numerator, sums, g_t):
    count = numerator.shape[1]
    lined = jnp.sum(g_t.astype(F32) * numerator, axis=0, keepdims=True)
    return jnp.concatenate(
        [
            numerator,
            jnp.zeros((WIDTH, count), F32),
            jnp.broadcast_to(sums, (8, count)),
            jnp.broadcast_to(lined, (24, count)),
        ],
        axis=0,
    )


def sum_rows(numerator, sums, g_t):
    return sum_columns(numerator, sums, g_t).T


def query_rows(part_t):
    count = part_t.shape[1]
    return jnp.concatenate([jnp.zeros((WIDTH, count), F32), part_t * SCALE, jnp.zeros((32, count), F32)], axis=0).T


def with_sums(picked, total, dots):
    large, small = total > 2.0**60, total < 2.0**-60
    level = jnp.where(large, 2.0**64, jnp.where(small, 2.0**-64, 1.0))
    unlevel = jnp.where(large, 2.0**-64, jnp.where(small, 2.0**64, 1.0))
    lane = lax.broadcasted_iota(jnp.int32, picked.shape, 1)
    for place, column in enumerate((*thirds(total * unlevel), level, *thirds(dots))):
        picked = jnp.where(lane == TD + place, column, picked)
    return picked.astype(BF16)


def fold(rows):
    tail = rows[:, 128:]
    pairs = jnp.concatenate([tail[:32, :64], tail[32:64, :64]], axis=1)
    sums = [tail[16 * i : 16 * i + 16, 64:72] for i in range(4)]
    last = jnp.concatenate([tail[64:, :72], *sums, jnp.zeros((16, 24), rows.dtype)], axis=1)
    return jnp.concatenate([rows[:, :128], pairs, last], axis=0)


def unfold(block):
    pairs, last = block[80:112], block[112:]
    tail = jnp.concatenate([pairs[:, :64], pairs[:, 64:]], axis=0)
    sums = jnp.concatenate([last[:, 72 + 8 * i : 80 + 8 * i] for i in range(4)], axis=0)
    three = jnp.concatenate([block[:64], tail, sums, jnp.zeros((64, 56), block.dtype)], axis=1)
    four = jnp.concatenate([block[64:80], last[:, :72], jnp.zeros((16, 56), block.dtype)], axis=1)
    return three, four


def sums_beside(far):
    def column(place):
        return far[:, TD + place : TD + place + 1]

    return (column(0) + column(1) + column(2)) * column(3), column(4) + column(5) + column(6)


def near_sums(far_t):
    td = far_t[TD : TD + 8].astype(F32)
    return (td[0:1] + td[1:2] + td[2:3]) * td[3:4], td[4:5] + td[5:6] + td[6:7]


def pick(grad_part, value_part):
    lane = lax.broadcasted_iota(jnp.int32, grad_part.shape, 1)
    return jnp.where(lane < WIDTH, grad_part * SCALE, value_part * 0.25)


def widen(x):
    return jnp.concatenate([x, jnp.zeros((x.shape[0], 128 - x.shape[1]), F32)], axis=1)


def both(keep_ref, came_ref, j, low, high):
    return jnp.concatenate([keep_ref[j, low:high, :], came_ref[j, low:high, :]], axis=1)


def taken_kernel(off_ref, keep_ref, came_ref, taken_ref, base_ref):
    first = OWN * lax.axis_index("core")
    row = lax.broadcasted_iota(jnp.int32, (TAKEN, 512), 0)
    col = lax.broadcasted_iota(jnp.int32, (TAKEN, 512), 1)
    is_two, is_three = row < 64, row < 72
    start = jnp.where(is_two, 8 * row, jnp.where(is_three, 64 * (row - 64), 256 * (row - 72)))
    blocks = []
    rows = []
    for j in range(8):
        o2, o3, o4 = off_ref[0, first + j], off_ref[1, first + j], off_ref[2, first + j]
        target = start + jnp.where(is_two, o2, jnp.where(is_three, o3, o4))
        hit = jnp.where(col == target, 1.0, 0.0).astype(BF16)
        columns = both(keep_ref, came_ref, j, 0, TD)
        picked = dot_t(hit, columns)
        picked_t = turn(jnp.concatenate([picked.astype(BF16), jnp.zeros((128 - TAKEN, TD), BF16)], axis=0))
        kv_t = columns[: 2 * WIDTH]
        blocks.append((turn(kv_t), kv_t[WIDTH:], picked_t[2 * WIDTH : 3 * WIDTH]))
        rows.append((picked, picked_t[3 * WIDTH :]))
    for j, (numerator, sums) in enumerate(forward_units(blocks)):
        picked, g_t = rows[j]
        base = sum_rows(numerator, sums, g_t)[:TAKEN]
        base_ref[j] = base
        picked = jnp.concatenate([picked, jnp.zeros((TAKEN, FAR_LANES - TD), F32)], axis=1)
        total = base[:, DEN : DEN + 1]
        taken_ref[j] = with_sums(picked, total, base[:, LINED : LINED + 1] / total)


def middle_kernel(off_ref, in_ref, block2_ref, far_ref):
    head = OWN * lax.axis_index("core") + lax.axis_index(CHIPS)
    o2, o3, o4 = off_ref[0, head], off_ref[1, head], off_ref[2, head]
    two = jnp.concatenate([in_ref[s, :64, :] for s in range(OWN)], axis=0)
    two_t = turn(two)
    numerator, sums = forward_unit(two[:, : 2 * WIDTH], two_t[WIDTH : 2 * WIDTH], two_t[2 * WIDTH : 3 * WIDTH])
    block2_ref[...] = sum_rows(numerator, sums, two_t[3 * WIDTH : TD])

    rest = jnp.concatenate([in_ref[s, 64:, :] for s in range(OWN)], axis=0)
    row = lax.broadcasted_iota(jnp.int32, (PICK_FAR, 128), 0)
    col = lax.broadcasted_iota(jnp.int32, (PICK_FAR, 128), 1)
    four = row - PICK_THREE
    source = jnp.where(row < PICK_THREE, 16 * (row >> 3) + (row & 7), 16 * (four >> 1) + 8 + (four & 1))
    far = dot(jnp.where(col == source, 1.0, 0.0).astype(BF16), rest)
    total, dots = sums_beside(far)
    from2 = jnp.concatenate(
        [
            jnp.where((o3 & 7) == o2, block2_ref[pl.ds(o3 >> 3, PICK_THREE, stride=8), :], 0.0),
            jnp.where((o4 & 7) == o2, block2_ref[pl.ds(o4 >> 3, PICK_FOUR, stride=32), :], 0.0),
        ],
        axis=0,
    )
    lined = dots * total + from2[:, LINED : LINED + 1]
    total = total + from2[:, DEN : DEN + 1]
    low = fold(with_sums(far, total, lined / total))
    for s in range(8):
        far_ref[s] = low


def far_forward(far):
    far_t = turn(far)
    result = forward_unit(far[:, : 2 * WIDTH], far_t[WIDTH : 2 * WIDTH], far_t[2 * WIDTH : 3 * WIDTH])
    return far_t, sum_rows(*result, far_t[3 * WIDTH : TD])


def three_kernel(off_ref, all_ref, block3_ref, three_ref, four_ref):
    head = OWN * lax.axis_index("core") + lax.axis_index(CHIPS)
    o3, o4 = off_ref[1, head], off_ref[2, head]
    meet = (o4 & 63) == o3
    parts = [unfold(all_ref[j]) for j in range(8)]
    far3 = jnp.concatenate([part[0] for part in parts], axis=0)
    three_ref[...] = far3
    block3_ref[...] = far_forward(far3)[1]
    four = jnp.concatenate([part[1] for part in parts], axis=0).astype(F32)
    from3 = jnp.where(meet, block3_ref[pl.ds(o4 >> 6, 128, stride=4), :], 0.0)
    total, dots = sums_beside(four)
    lined = dots * total + from3[:, LINED : LINED + 1]
    total = total + from3[:, DEN : DEN + 1]
    four_ref[...] = with_sums(four, total, lined / total)


def totals_of(far_t, rows):
    near_total, near_dots = near_sums(far_t)
    far = rows.T
    total = near_total + far[DEN : DEN + 1]
    total = jnp.where(total > 0.0, total, 1.0)
    return 1.0 / (total * 0.25), (near_dots * near_total + far[LINED : LINED + 1]) / total


def ahead_kernel(in_ref, far3_ref, two_ref, two_t_ref, far3_t_ref, weights_ref, probs_ref):
    two = jnp.concatenate([in_ref[s, :64, :] for s in range(OWN)], axis=0)
    two_t = turn(two)
    two_ref[...] = two
    two_t_ref[...] = two_t
    far3_t_ref[...] = turn(far3_ref[...])
    kv = two[:, : 2 * WIDTH]
    weights_ref[...] = jnp.exp2(dot(kv, upper(two_t[2 * WIDTH : 3 * WIDTH])) * EXPONENT)
    probs_ref[...] = dot(kv, lower(two_t[3 * WIDTH : TD]))


def far_kernel(
    off_ref, two_in_ref, two_t_ref, far3_t_ref, weights_ref, probs_ref,
    block2_ref, far3_ref, block3_ref, here_ref, there_ref,
    out_ref, two_ref, three_ref, four_ref,
):
    head = OWN * lax.axis_index("core") + lax.axis_index(CHIPS)
    group = lax.axis_index(HALF)
    o2, o3, o4 = off_ref[0, head], off_ref[1, head], off_ref[2, head]
    meet = (o4 & 63) == o3
    own_rows3 = pl.ds(pl.multiple_of(group * PICK_THREE, PICK_THREE), PICK_THREE)
    own_rows4 = pl.ds(pl.multiple_of(group * PICK_FOUR, PICK_FOUR), PICK_FOUR)

    far3 = far3_ref[...]
    far3_t = far3_t_ref[...]
    far4 = jnp.concatenate([here_ref[...], there_ref[...]], axis=0)
    far4_t, block4 = far_forward(far4)
    four_ref[...] = block4
    three_ref[...] = block3_ref[...]
    same = pl.ds(o4 >> 6, 128, stride=4)
    three_ref[same, :] = three_ref[same, :] + jnp.where(meet, four_ref[:128, :], 0.0)

    own3 = three_ref[own_rows3, :]
    own4 = four_ref[own_rows4, :]
    only4 = jnp.where(meet, 0.0, own4)
    two_ref[...] = block2_ref[...]
    in_two = pl.ds(o3 >> 3, PICK_THREE, stride=8)
    two_ref[in_two, :] = two_ref[in_two, :] + jnp.where((o3 & 7) == o2, own3, 0.0)
    in_two = pl.ds(o4 >> 3, PICK_FOUR, stride=32)
    two_ref[in_two, :] = two_ref[in_two, :] + jnp.where((o4 & 7) == o2, only4, 0.0)

    two = two_in_ref[...]
    two_t = two_t_ref[...]
    pad = 128 - PICK_FAR
    own = jnp.concatenate(
        [far3_ref[own_rows3, :], here_ref[own_rows4, :], jnp.zeros((pad, FAR_LANES), BF16)], axis=0
    )
    own_t = turn(own)
    own_block = jnp.concatenate([own3, own4, jnp.zeros((pad, 128), F32)], axis=0)
    inverse2, dots2 = totals_of(two_t, two_ref[...])
    inverse3, dots3 = totals_of(far3_t, three_ref[...])
    inverse4, dots4 = totals_of(far4_t, four_ref[...])
    own_inverse, own_dots = totals_of(own_t, own_block)

    def queries(turned):
        return turned[2 * WIDTH : 3 * WIDTH], turned[3 * WIDTH : TD]

    kv_own = own[:, : 2 * WIDTH]
    shares2 = weights_ref[...] * inverse2
    result2 = (shares2.astype(BF16), (shares2 * (probs_ref[...] - dots2)).astype(BF16))
    results = [result2] + backward_units((
        (far3[:, : 2 * WIDTH], *queries(own_t), own_inverse, own_dots),
        (far4[:, : 2 * WIDTH], *queries(own_t), own_inverse, own_dots),
        (kv_own, *queries(far3_t), inverse3, dots3),
        (kv_own, *queries(far4_t), inverse4, dots4),
    ))
    query2 = query_rows(dot(two_t[:WIDTH], results[0][1])) + block2_ref[...]
    query3 = query_rows(dot(far3_t[:WIDTH], results[1][1]))[:PICK_THREE] + own3
    query4 = query_rows(dot(far4_t[:WIDTH], results[2][1]))[PICK_THREE:PICK_FAR] + only4

    def keys(result, far):
        qg = far[:, 2 * WIDTH : TD]
        return widen(pick(dot(result[1], qg), dot(result[0], qg)))

    keys2 = keys(results[0], two)
    keys3 = keys(results[3], far3)[:PICK_THREE]
    keys4 = keys(results[4], far4)[PICK_THREE:PICK_FAR]
    for lanes, part2, part3, part4 in (
        (slice(0, 128), keys2, keys3, keys4),
        (slice(128, 256), query2, query3, query4),
    ):
        for c in range(OWN):
            out_ref[c, :64, lanes] = part2[64 * c : 64 * c + 64]
            out_ref[c, 64:72, lanes] = part3[8 * c : 8 * c + 8]
            out_ref[c, 72:74, lanes] = part4[2 * c : 2 * c + 2]
            out_ref[c, 74:, lanes] = jnp.zeros((TAKEN - 74, 128), F32)


def lone_kernel(first_step, off_ref, keep_ref, came_ref, *refs):
    near_ref, keys_ref = refs[-2:]
    first = OWN * lax.axis_index("core") + 2 * (first_step + pl.program_id(0))
    blocks = []
    for j in range(2):
        kv_t = both(keep_ref, came_ref, j, 0, 2 * WIDTH)
        qg_t = both(keep_ref, came_ref, j, 2 * WIDTH, TD)
        blocks.append((turn(kv_t), kv_t, qg_t, turn(qg_t)))
    scores = [dot(kv, upper(qg_t[:WIDTH])) for kv, _, qg_t, _ in blocks]
    probs = [dot(kv, lower(qg_t[WIDTH:])) for kv, _, qg_t, _ in blocks]
    weights = [jnp.exp2(score * EXPONENT) for score in scores]
    shares = []
    for j, weight in enumerate(weights):
        inverse = 1.0 / (jnp.sum(weight, axis=0, keepdims=True) * 0.25)
        shares.append(weight * jnp.where(chosen_columns(off_ref, first + j), 0.0, inverse))
    low = [share.astype(BF16) for share in shares]
    merged = [dot(block[1][WIDTH:], share) * 0.25 for block, share in zip(blocks, low)]
    dots = [
        jnp.sum(block[2][WIDTH:].astype(F32) * part, axis=0, keepdims=True) for block, part in zip(blocks, merged)
    ]
    grads = [(share * (prob - line)).astype(BF16) for share, prob, line in zip(shares, probs, dots)]
    query_parts = [dot(block[1][:WIDTH], grad) * SCALE for block, grad in zip(blocks, grads)]
    grad_parts = [dot(grad, block[3]) for block, grad in zip(blocks, grads)]
    value_parts = [dot(share, block[3]) for block, share in zip(blocks, low)]
    for j in range(2):
        near_ref[j, :WIDTH, :] = merged[j].astype(BF16)
        near_ref[j, WIDTH:, :] = query_parts[j].astype(BF16)
        keys_ref[j * 512 : j * 512 + 512, :] = widen(pick(grad_parts[j], value_parts[j]))


def lone_half(first_step, offsets, keep, came, filled):
    def spec(*shape):
        return pl.BlockSpec(shape, lambda i: (first_step + i,) + (0,) * (len(shape) - 1))

    heads = spec(2, 4 * WIDTH, ROWS)
    return pl.pallas_call(
        functools.partial(lone_kernel, first_step),
        out_shape=(pltpu.HBM((OWN, 2 * WIDTH, 512), BF16), pltpu.HBM((GROUP_ROWS, 128), F32)),
        grid=(2,),
        in_specs=[pl.BlockSpec(memory_space=pltpu.SMEM), heads, heads]
        + [pl.BlockSpec(memory_space=pl.ANY)] * len(filled),
        out_specs=(spec(2, 2 * WIDTH, 512), spec(1024, 128)),
        input_output_aliases={3 + place: place for place in range(len(filled))},
        compiler_params=pltpu.CompilerParams(vmem_limit_bytes=LIMIT),
    )(offsets, keep, came, *filled)


def chosen_columns(off_ref, head):
    col = lax.broadcasted_iota(jnp.int32, (1, 512), 1)
    two = (col & 7) == off_ref[0, head]
    three = (col & 63) == off_ref[1, head]
    four = (col & 255) == off_ref[2, head]
    return jnp.logical_or(two, jnp.logical_or(three, four))


def last_backward_kernel(
    off_ref, keep_ref, came_ref, taken_ref, base_ref, back_ref, near_ref, lone_ref,
    stay_ref, leave_ref, rows_ref, keys_ref,
):
    first = OWN * lax.axis_index("core") + 4 * pl.program_id(0)
    rows_b = slice(128, 256)

    def put(j, low, high, value):
        stay_ref[j, low:high, :] = value[:, :ROWS]
        leave_ref[j, low:high, :] = value[:, ROWS:]

    def valid(place, three_in_two, four_in_more):
        is_three = jnp.logical_and(place >= 64, place < 72)
        is_four = jnp.logical_and(place >= 72, place < 74)
        lost = jnp.where(is_three, three_in_two, jnp.where(is_four, four_in_more, jnp.where(place < 64, 0, 1)))
        return lost == 0

    blocks = []
    rest = []
    for j in range(4):
        o2, o3, o4 = off_ref[0, first + j], off_ref[1, first + j], off_ref[2, first + j]
        three_in_two = (o3 & 7) == o2
        four_in_two = (o4 & 7) == o2
        meet = (o4 & 63) == o3
        only_three = jnp.logical_and(meet, jnp.logical_not(four_in_two))
        flags = (three_in_two.astype(jnp.int32), jnp.logical_or(meet, four_in_two).astype(jnp.int32))
        rows_ref[j, TAKEN:, :] = jnp.ones((128 - TAKEN, 128), F32)
        rows_ref[j, :TAKEN, :] = base_ref[j] + back_ref[j, :, rows_b]
        for rows, low, high, take in (
            (pl.ds(o3 >> 3, 8, stride=8), 64, 72, three_in_two),
            (pl.ds(o4 >> 3, 2, stride=32), 72, 74, four_in_two),
            (pl.ds(64 + (o4 >> 6), 2, stride=4), 72, 74, only_three),
        ):
            rows_ref[j, rows, :] = rows_ref[j, rows, :] + jnp.where(take, back_ref[j, low:high, rows_b], 0.0)
        sums = rows_ref[j].T
        total = sums[DEN : DEN + 1]
        lane = lax.broadcasted_iota(jnp.int32, (1, 128), 1)
        inverse = jnp.where(valid(lane, *flags), 1.0 / (total * 0.25), 0.0)
        taken = jnp.concatenate([taken_ref[j], jnp.zeros((128 - TAKEN, FAR_LANES), BF16)], axis=0)
        taken_t = turn(taken)
        kv_t = both(keep_ref, came_ref, j, 0, 2 * WIDTH)
        blocks.append((
            turn(kv_t), taken_t[2 * WIDTH : 3 * WIDTH], taken_t[3 * WIDTH : TD], inverse,
            sums[LINED : LINED + 1] / total,
        ))
        row = lax.broadcasted_iota(jnp.int32, (128, 512), 0)
        col = lax.broadcasted_iota(jnp.int32, (128, 512), 1)
        target = jnp.where(row < 64, 8 * row + o2, jnp.where(row < 72, 64 * (row - 64) + o3, 256 * (row - 72) + o4))
        hit = jnp.logical_and(col == target, valid(row, *flags))
        rest.append((
            kv_t[:WIDTH], taken[:, 2 * WIDTH : TD], sums[:WIDTH] / total, sums[WIDTH : 2 * WIDTH],
            jnp.where(hit, 1.0, 0.0).astype(BF16),
        ))
    results = backward_units(blocks)
    query_parts = [dot(part[0], grad) * SCALE + part[3] for part, (_, grad) in zip(rest, results)]
    grad_parts = [dot(grad, part[1]) for part, (_, grad) in zip(rest, results)]
    value_parts = [dot(share, part[1]) for part, (share, _) in zip(rest, results)]
    for j in range(4):
        low = jnp.concatenate([rest[j][2], query_parts[j]], axis=0).astype(BF16)
        spread = dot(low, rest[j][4])
        chosen = chosen_columns(off_ref, first + j)
        put(j, 0, 2 * WIDTH, jnp.where(chosen, spread, near_ref[j].astype(F32)).astype(BF16))
        base = j * 512
        keys_ref[base : base + 512, :] = lone_ref[base : base + 512, :] + widen(pick(grad_parts[j], value_parts[j]))
        for low, high, which, stride in ((0, 64, 0, 8), (64, 72, 1, 64), (72, 74, 2, 256)):
            rows = pl.ds(base + off_ref[which, first + j], high - low, stride=stride)
            keys_ref[rows, :] = keys_ref[rows, :] + back_ref[j, low:high, :128]
        put(j, 2 * WIDTH, TD, keys_ref[base : base + 512, :].astype(BF16).T[: 2 * WIDTH])


def per_device(queries, key_states, value_states, cotangent, offsets):
    struct = jax.ShapeDtypeStruct

    def in_hbm(x):
        return pltpu.with_memory_space_constraint(x, pltpu.HBM)

    def in_vmem(x):
        return pltpu.with_memory_space_constraint(x, pltpu.VMEM)

    queries, key_states, value_states, cotangent, offsets = map(
        in_hbm, (queries, key_states, value_states, cotangent, offsets)
    )
    def swap(x):
        return lax.ppermute(x, "core", [(0, 1), (1, 0)])

    half = struct((OWN, 4 * WIDTH, ROWS), BF16)
    arrays = (key_states, value_states, queries, cotangent)
    came = swap(pack_half(arrays, False, half))
    keep = pack_half(arrays, True, half)
    rows_f32 = pltpu.HBM((GROUP_ROWS, 128), F32)
    picked, base = call(
        taken_kernel,
        (struct((OWN, TAKEN, FAR_LANES), BF16), pltpu.HBM((OWN, TAKEN, 128), F32)),
        steps=0,
        smem=1,
        args=(offsets, keep, came),
    )
    taken = in_vmem(lax.all_to_all(picked, CHIPS, 0, 0, tiled=True))
    near, lone = lone_half(0, offsets, keep, came, ())
    taken, near, lone = lax.optimization_barrier((taken, near, lone))
    block2, far = call(
        middle_kernel,
        (struct((PICK_TWO, 128), F32), struct((8, 128, 128), BF16)),
        smem=1,
        args=(offsets, taken),
    )
    far = lax.all_to_all(far, HALF, 0, 0, tiled=True)
    block3, far3, here = call(
        three_kernel,
        (struct((512, 128), F32), struct((512, FAR_LANES), BF16), struct((128, FAR_LANES), BF16)),
        smem=1,
        args=(offsets, far),
    )
    there = lax.ppermute(here, "y_high", [(0, 1), (1, 0)])
    square = struct((512, 512), F32)
    turned = struct((FAR_LANES, 512), BF16)
    ahead = call(
        ahead_kernel,
        (struct((512, FAR_LANES), BF16), turned, turned, square, square),
        args=(taken, far3),
    )
    back = call(
        far_kernel,
        struct((OWN, TAKEN, 256), F32),
        scratch=(pltpu.VMEM((512, 128), F32), pltpu.VMEM((512, 128), F32), pltpu.VMEM((256, 128), F32)),
        smem=1,
        args=(offsets, *ahead, block2, far3, block3, here, there),
    )
    back = in_vmem(lax.all_to_all(back, CHIPS, 0, 0, tiled=True))
    near, lone = lone_half(2, offsets, keep, came, (in_hbm(near), in_hbm(lone)))
    stay, leave = call(
        last_backward_kernel,
        (half, half),
        scratch=(pltpu.VMEM((4, 128, 128), F32), pltpu.VMEM((2048, 128), F32)),
        steps=2,
        smem=1,
        args=(offsets, keep, came, picked, in_hbm(base), back, in_hbm(near), in_hbm(lone)),
    )
    came = swap(leave)
    outs = unpack_half(stay, True, ())
    return tuple(unpack_half(came, False, tuple(map(in_hbm, outs))))


def solution(mesh):
    axes = ("y_high", "y_low", "z_high", "z_low", "x", "core")
    inner = Mesh(mesh.devices.reshape(2, 2, 4, 2, 4, 2), axes)
    rows = P(axes, None)
    return jax.shard_map(
        per_device,
        mesh=inner,
        in_specs=(rows, rows, rows, rows, P()),
        out_specs=(rows, rows, rows, rows),
        check_vma=False,
    )
```
